32 devices in a mesh: ent: 8 (over z, y), sec: 4 (over x, core).
Axes of the slice: x: 2, y: 2, z: 4, core: 2. Of those that a mesh axis runs over, the one named last changes fastest.
Arguments:
- features: bfloat16 [1024, 256], P('ent'), may hold values from -6 to 6
- theta: bfloat16 [256, 256], replicated, may hold values from -3 to 3
- section_weight: float32 [16384], P(('ent', 'sec')), may hold values from 0.5 to 2
- pair_rows: int32 [32, 8, 512], P(('ent', 'sec')), may hold values from 0 to 511
- pair_cols: int32 [32, 8, 512], P(('ent', 'sec')), may hold values from 0 to 127
- pair_counts: int32 [32, 8], P(('ent', 'sec')), may hold values from 0 to 512, as said below
- cotangent: bfloat16 [1024, 256], P('ent'), may hold values from -24 to 24
Outputs:
- activated: bfloat16 [1024, 256], P('ent')
- grad_features: bfloat16 [1024, 256], P('ent')
- grad_theta: float32 [256, 256], replicated
- grad_weight: float32 [16384], P(('ent', 'sec'))
The draws below stay inside these ranges and needn't reach their ends.
Inputs may be any that keep to these rules, and one draw needn't show every extreme that they name: Only the first pair_counts[k, j] slots of shard k and block j are used; some shard uses all 512 slots of some block.
All inputs are finite; a program needn't handle non-finite values.
Results may differ from the reference program's by a relative error of at most 0.0059.
Values may be sent and summed in bfloat16 or wider, within the bound.
No kernel may reach another device: no remote copies, remote signals or barrier semaphores. Data moves between devices by JAX's collectives and lax.ppermute only.
A program may use at most 64 MiB of HBM per device.

```python
import math
import jax
import jax.numpy as jnp
from jax import lax

F = 256
ENT_DEV = 128
SEC_DEV = 512
PAIRS = 512
ENTS = 1024
SHARDS = 32
SECTIONS = 16384
N_ENT = 8


def draw_pair_counts(key, part):
    level_key, hot_key, jitter_key, full_key = jax.random.split(key, 4)
    levels = jax.random.randint(level_key, (N_ENT,), 0, 4)
    hot_block = jax.random.randint(hot_key, (), 0, N_ENT)
    block_ids = jnp.arange(N_ENT, dtype=jnp.int32)
    levels = jnp.where(block_ids == hot_block, 3, levels)
    block_load = PAIRS * jnp.left_shift(jnp.int32(1), levels) // 8
    jitter = jax.random.randint(jitter_key, (SHARDS, N_ENT), 0, PAIRS // 16 + 1)
    full_shard = jax.random.randint(full_key, (), 0, SHARDS)
    shard_ids = jnp.arange(SHARDS, dtype=jnp.int32)
    pinned = (shard_ids[:, None] == full_shard) & (block_ids[None, :] == hot_block)
    jitter = jnp.where(pinned, 0, jitter)
    return jnp.maximum(block_load[None, :] - jitter, 0).astype(jnp.int32)


def touch_ends(result, key, smallest, high):
    extent = result.shape
    index_at = [jax.random.randint(jax.random.fold_in(key, axis), (), 0, extent[axis]) for axis in range(len(extent))]
    result = result.at[tuple(index_at)].set(smallest)
    longest = extent.index(max(extent))
    index_at[longest] = (index_at[longest] + 1) % extent[longest]
    return result.at[tuple(index_at)].set(high)


def steps_of(rng, dims, cuts, least, top_value):
    level = 1.0
    for dim, blocks in cuts:
        draws = jax.random.uniform(jax.random.fold_in(jax.random.fold_in(rng, 6), dim), (blocks,), jnp.float32, least / len(cuts), top_value / len(cuts))
        level = level * jnp.repeat(jnp.exp(draws), dims[dim] // blocks).reshape((-1,) + (1,) * (len(dims) - 1 - dim))
    return level


def centred(own_key, extent, scale, bound, cuts=(), kind=jnp.bfloat16):
    drawn = jax.random.normal(own_key, extent, jnp.float32) * scale
    if len(cuts) > 0:
        drawn = steps_of(own_key, extent, cuts, -0.22, 0.18) * drawn
    return jnp.clip(drawn, min=-bound, max=bound).astype(kind)


def setup_inputs(seed: int = 0) -> dict:
    streams_of = jax.random.split(jax.random.key(seed), 8)
    features = centred(streams_of[0], (ENTS, F), 1.0, 6.0, ((0, 8),))
    theta = centred(streams_of[1], (F, F), 0.5, 3.0)
    section_weight = jnp.clip(jnp.exp(math.log(2.0) - 1.3862944 * jax.random.uniform(streams_of[2], (SECTIONS,), jnp.float32) ** steps_of(streams_of[2], (SECTIONS,), ((0, 32),), -0.2, 0.2)), 0.5, 2.0)
    pair_rows = touch_ends(jax.random.randint(streams_of[3], (SHARDS, N_ENT, PAIRS), 0, SEC_DEV), jax.random.fold_in(streams_of[3], 1), 0, SEC_DEV - 1).astype(jnp.int32)
    pair_cols = touch_ends(jax.random.randint(streams_of[4], (SHARDS, N_ENT, PAIRS), 0, ENT_DEV), jax.random.fold_in(streams_of[4], 1), 0, ENT_DEV - 1).astype(jnp.int32)
    pair_counts = draw_pair_counts(jax.random.fold_in(streams_of[7], 71), 0)
    cotangent = centred(streams_of[6], (ENTS, F), 4.0, 24.0, ((0, 8),))
    return {"features": features, "theta": theta, "section_weight": section_weight, "pair_rows": pair_rows, "pair_cols": pair_cols, "pair_counts": pair_counts, "cotangent": cotangent}


def reference(features, theta, section_weight, pair_rows, pair_cols, pair_counts, cotangent):
    shards, blocks_count, slot_count = pair_rows.shape
    usable = (jnp.arange(slot_count, dtype=jnp.int32)[None, None, :] < pair_counts[:, :, None]).astype(jnp.float32)
    entity_index = (jnp.arange(blocks_count, dtype=jnp.int32)[None, :, None] * ENT_DEV + pair_cols).reshape(shards, -1).astype(jnp.int32)
    row_index = pair_rows.reshape(shards, -1).astype(jnp.int32)
    usable_flat = usable.reshape(shards, -1)
    entity_degree = jnp.zeros((ENTS,), jnp.float32).at[entity_index.reshape(-1)].add(usable_flat.reshape(-1))
    entity_scale = lax.rsqrt(1.0 + entity_degree)[:, None]

    def count_rows(rows_here, live_here):
        return jnp.zeros((SEC_DEV,), jnp.float32).at[rows_here].add(live_here)
    sec_count = jax.vmap(count_rows)(row_index, usable_flat).reshape(-1)
    section_scale = (section_weight / (1.0 + sec_count))[:, None]

    def gather_sections(values):

        def per_shard(packed):
            rows_here, cols_here, live_here = packed
            picked = values[cols_here].astype(jnp.float32) * live_here[:, None]
            return jnp.zeros((SEC_DEV, values.shape[1]), jnp.float32).at[rows_here].add(picked)
        return lax.map(per_shard, (row_index, entity_index, usable_flat)).reshape(-1, values.shape[1])

    def scatter_entities(messages):
        shard_rows = messages.reshape(shards, SEC_DEV, -1)

        def add_shard(running, packed):
            rows_here, cols_here, live_here, rows_block = packed
            picked = rows_block[rows_here].astype(jnp.float32) * live_here[:, None]
            return (running.at[cols_here].add(picked), None)
        running, _ = lax.scan(add_shard, jnp.zeros((ENTS, messages.shape[1]), jnp.float32), (row_index, entity_index, usable_flat, shard_rows))
        return running
    projected = jnp.dot(features, theta, preferred_element_type=jnp.float32)
    scaled = (entity_scale * projected).astype(jnp.bfloat16)
    gathered = gather_sections(scaled)
    messages = (section_scale * gathered).astype(jnp.bfloat16)
    collected = scatter_entities(messages)
    preact = entity_scale * collected
    activated = jax.nn.silu(preact).astype(jnp.bfloat16)
    sigmoid_pre = jax.nn.sigmoid(preact)
    grad_pre = cotangent.astype(jnp.float32) * sigmoid_pre * (1.0 + preact * (1.0 - sigmoid_pre))
    back_scaled = (entity_scale * grad_pre).astype(jnp.bfloat16)
    back_gathered = gather_sections(back_scaled)
    grad_weight = lax.optimization_barrier(jnp.sum(gathered * back_gathered, axis=1)) / (1.0 + sec_count)
    back_messages = (section_scale * back_gathered).astype(jnp.bfloat16)
    back_collected = scatter_entities(back_messages)
    grad_proj = (entity_scale * back_collected).astype(jnp.bfloat16)
    grad_features = jnp.dot(grad_proj, theta.T, preferred_element_type=jnp.float32).astype(jnp.bfloat16)
    grad_theta = jnp.dot(features.T, grad_proj, preferred_element_type=jnp.float32)
    return (activated, grad_features, grad_theta, grad_weight)
```

```python
import jax
import jax.numpy as jnp
from jax import lax
from jax.experimental import pallas as pl
from jax.experimental.pallas import tpu as pltpu
from jax.sharding import Mesh, PartitionSpec as P


def hot_table(indices, live_slots, offset, table_width):
    hits = (indices - offset)[:, None] == jnp.arange(table_width, dtype=jnp.int32)[None, :]
    return (hits & live_slots[:, None]).astype(jnp.bfloat16)


def body(features, theta, section_weight, pair_rows, pair_cols, pair_counts, cotangent):
    ent_dev = features.shape[0]
    feature_width = features.shape[1]
    sec_dev = section_weight.shape[0]
    blocks_count = pair_rows.shape[1]
    slot_count = pair_rows.shape[2]
    own_block = lax.axis_index("ent")
    row_lists = pair_rows[0]
    col_lists = pair_cols[0]
    usable = jnp.arange(slot_count, dtype=jnp.int32)[None, :] < pair_counts[0][:, None]
    usable_float = usable.astype(jnp.float32)
    entity_index = jnp.arange(blocks_count, dtype=jnp.int32)[:, None] * ent_dev + col_lists
    local_degree = jax.ops.segment_sum(
        usable_float.reshape(-1), entity_index.reshape(-1), num_segments=blocks_count * ent_dev
    )
    entity_degree = lax.psum(local_degree, ("ent", "sec"))
    own_degree = lax.dynamic_slice_in_dim(entity_degree, own_block * ent_dev, ent_dev)
    entity_scale = lax.rsqrt(1.0 + own_degree)[:, None]
    sec_count = jax.ops.segment_sum(
        usable_float.reshape(-1), row_lists.reshape(-1), num_segments=sec_dev
    )
    section_scale = (section_weight / (1.0 + sec_count))[:, None]

    def entity_fold(running, incoming, start_row):
        row_count = incoming.shape[0]
        span_width = min(row_count, ent_dev)
        block_span = max(row_count // ent_dev, 1)
        offset = start_row

        def add_block(turn_index, accum):
            row_slots = lax.dynamic_index_in_dim(row_lists, turn_index, 0, keepdims=False)
            col_slots = lax.dynamic_index_in_dim(col_lists, turn_index, 0, keepdims=False)
            live_slots = lax.dynamic_index_in_dim(usable, turn_index, 0, keepdims=False)
            values = lax.dynamic_slice_in_dim(incoming, turn_index * span_width, span_width, 0)
            col_hot = hot_table(col_slots, live_slots, offset, span_width)
            row_hot = hot_table(row_slots, live_slots, 0, sec_dev)
            picked = jnp.dot(col_hot, values, preferred_element_type=jnp.float32).astype(
                jnp.bfloat16
            )
            return accum + jnp.einsum(
                "ps,pf->sf", row_hot, picked, preferred_element_type=jnp.float32
            )

        return lax.fori_loop(0, block_span, add_block, running)

    def entity_terms(messages, start_row):
        span_width = min(lax.axis_size("ent") * ent_dev, ent_dev)
        block_span = max(lax.axis_size("ent") * ent_dev // ent_dev, 1)
        offset = start_row

        def block_term(turn_index):
            row_slots = lax.dynamic_index_in_dim(row_lists, turn_index, 0, keepdims=False)
            col_slots = lax.dynamic_index_in_dim(col_lists, turn_index, 0, keepdims=False)
            live_slots = lax.dynamic_index_in_dim(usable, turn_index, 0, keepdims=False)
            row_hot = hot_table(row_slots, live_slots, 0, sec_dev)
            col_hot = hot_table(col_slots, live_slots, offset, span_width)
            picked = jnp.dot(row_hot, messages, preferred_element_type=jnp.float32).astype(
                jnp.bfloat16
            )
            return jnp.einsum("pw,pf->wf", col_hot, picked, preferred_element_type=jnp.float32)

        pieces = lax.map(block_term, jnp.arange(block_span, dtype=jnp.int32))
        return pieces.reshape(block_span * span_width, feature_width)

    def collect(messages):
        partial_sum = lax.psum_scatter(
            entity_terms(messages, jnp.int32(0)), "ent", scatter_dimension=0, tiled=True
        )
        return lax.psum(partial_sum, "sec")

    zero_sections = jnp.zeros((sec_dev, feature_width), jnp.float32)
    projected = jnp.dot(features, theta, preferred_element_type=jnp.float32)
    scaled = (entity_scale * projected).astype(jnp.bfloat16)
    gathered = entity_fold(
        zero_sections, lax.all_gather(scaled, "ent", axis=0, tiled=True), jnp.int32(0)
    )
    messages = (section_scale * gathered).astype(jnp.bfloat16)
    collected = collect(messages)
    preact = entity_scale * collected
    activated = jax.nn.silu(preact).astype(jnp.bfloat16)
    sigmoid_pre = jax.nn.sigmoid(preact)
    grad_pre = cotangent.astype(jnp.float32) * sigmoid_pre * (1.0 + preact * (1.0 - sigmoid_pre))
    back_scaled = (entity_scale * grad_pre).astype(jnp.bfloat16)
    back_gathered = entity_fold(
        zero_sections, lax.all_gather(back_scaled, "ent", axis=0, tiled=True), jnp.int32(0)
    )
    grad_weight = jnp.sum(gathered * back_gathered, axis=1) / (1.0 + sec_count)
    back_messages = (section_scale * back_gathered).astype(jnp.bfloat16)
    back_collected = collect(back_messages)
    grad_proj = (entity_scale * back_collected).astype(jnp.bfloat16)
    grad_features = lax.dot_general(
        grad_proj, theta, (((1,), (1,)), ((), ())), preferred_element_type=jnp.float32
    ).astype(jnp.bfloat16)
    local_theta = lax.dot_general(
        features, grad_proj, (((0,), (0,)), ((), ())), preferred_element_type=jnp.float32
    )
    grad_theta = lax.psum(local_theta, "ent")
    return (activated, grad_features, grad_theta, grad_weight)


BF = jnp.bfloat16
F32 = jnp.float32
TILE = 256
NT = (((1,), (1,)), ((), ()))
TN = (((0,), (0,)), ((), ()))


def params():
    return pltpu.CompilerParams(vmem_limit_bytes=48 * 2**20)


def vmem():
    return pl.BlockSpec(memory_space=pltpu.VMEM)


def dot(a, b, dims=(((1,), (0,)), ((), ()))):
    return lax.dot_general(a, b, dims, preferred_element_type=F32)


def one_hot(index_row):
    ids = lax.broadcasted_iota(jnp.int32, (TILE, index_row.shape[1]), 0).astype(BF)
    return jnp.where(ids == index_row, jnp.ones((), BF), jnp.zeros((), BF))


def column_to_row(column):
    wide = jnp.broadcast_to(column, (column.shape[0], 128))
    return wide.T[0:1, :]


def row_to_column(row):
    return jnp.broadcast_to(row, (128, 128)).T


def prep_kernel(counts, rows, cols, weight, payload, incidence, inverse):
    copies, _, slots = payload.shape
    blocks = rows.shape[1]
    ent_dev = incidence.shape[1] // blocks
    row_ids = rows[0]
    col_ids = cols[0]
    sub = lax.broadcasted_iota(jnp.int32, (blocks, slots), 0)
    lane = lax.broadcasted_iota(jnp.int32, (blocks, slots), 1)
    limit = jnp.zeros((blocks, slots), jnp.int32)
    for j in range(blocks):
        limit = jnp.where(sub == j, counts[0, j], limit)
    live = lane < limit
    high = jnp.where(live, (row_ids // TILE) * ent_dev + col_ids, -1).astype(F32)
    low = jnp.where(live, row_ids % TILE, -1).astype(F32)
    totals = [jnp.zeros((TILE, ent_dev), F32) for _ in range(2)]
    for j in range(blocks):
        high_hot = one_hot(high[j : j + 1].astype(BF))
        low_hot = one_hot(low[j : j + 1].astype(BF))
        block = dot(low_hot, high_hot, NT)
        for half in range(2):
            part = block[:, half * ent_dev : (half + 1) * ent_dev]
            totals[half] = totals[half] + part
            incidence[half * TILE : (half + 1) * TILE, j * ent_dev : (j + 1) * ent_dev] = part.astype(BF)
    degree = jnp.concatenate(
        [column_to_row(jnp.sum(t, axis=1, keepdims=True)) for t in totals], axis=1
    )
    inv = 1.0 / (1.0 + degree)
    inverse[...] = inv
    scale = weight[...] / (1.0 + degree)
    message = jnp.concatenate(
        [high, low, jnp.broadcast_to(scale, (blocks, slots))], axis=0
    ).astype(BF)
    for n in range(copies):
        payload[n] = message


def gram_kernel(lists, gram, table, scaled, *sums):
    shards, _, slots = lists.shape
    ents = table.shape[0]
    blocks = (lists.shape[1]) // 3
    ent_dev = ents // blocks
    tiles = ents // TILE
    for acc in sums:
        acc[...] = jnp.zeros_like(acc)
    scaled[ents:, :] = jnp.ones((scaled.shape[0] - ents, scaled.shape[1]), BF)

    def shard(k, carry):
        indices = lists[k]
        for j in range(blocks):
            high_hot = one_hot(indices[j : j + 1])
            low_hot = one_hot(indices[blocks + j : blocks + j + 1])
            block = dot(high_hot, low_hot, NT).astype(BF)
            for half in range(2):
                table[j * ent_dev : (j + 1) * ent_dev, half * TILE : (half + 1) * TILE] = block[
                    half * ent_dev : (half + 1) * ent_dev, :
                ]
        scale = indices[2 * blocks : 2 * blocks + 1]
        scaled[0:ents, :] = table[...] * scale
        for b in range(tiles):
            sums[b][...] += dot(
                scaled[b * TILE :, :], table[b * TILE : (b + 1) * TILE, :], NT
            )
        return carry

    lax.fori_loop(0, shards, shard, 0)
    start = 0
    degrees = []
    for b in range(tiles):
        size = ents - b * TILE
        gram[start : start + size, :] = sums[b][0:size, :].astype(BF)
        start += size
        degree = sums[b][size : size + 1, :]
        top = degree.astype(BF)
        degrees.append(top.astype(F32))
        degrees.append(degree - top.astype(F32))
    degrees.append(jnp.zeros((16 - 2 * tiles, TILE), F32))
    gram[start : start + 16, :] = jnp.concatenate(degrees, axis=0).astype(BF)


def tail_kernel(
    own, other, gathered, theta, incidence, inverse,
    activated, grad_features, grad_theta, grad_weight,
    full, scale, values, backs, acts, projs,
):
    ents = full.shape[0]
    tiles = ents // TILE
    ent_dev = activated.shape[0]
    groups = ents // ent_dev
    width = theta.shape[0]
    core = lax.axis_index("core")
    mine = lax.axis_index("ent")
    base = sum(ents - b * TILE for b in range(tiles))
    degree_rows = own[base : base + 16, :].astype(F32) + other[base : base + 16, :].astype(F32)
    for b in range(tiles):
        row = lax.rsqrt(1.0 + (degree_rows[2 * b : 2 * b + 1] + degree_rows[2 * b + 1 : 2 * b + 2]))
        for h in range(TILE // 128):
            at = b * TILE + h * 128
            scale[at : at + 128, :] = row_to_column(row[:, h * 128 : (h + 1) * 128])
    for which, source in enumerate((own, other)):
        column = (core if which == 0 else 1 - core) * ents
        start = 0
        for b in range(tiles):
            for a in range(b, tiles):
                piece = source[start : start + TILE, :]
                full[a * TILE : (a + 1) * TILE, pl.ds(pl.multiple_of(column + b * TILE, TILE), TILE)] = piece
                if a != b:
                    full[b * TILE : (b + 1) * TILE, pl.ds(pl.multiple_of(column + a * TILE, TILE), TILE)] = piece.T
                start += TILE

    def es(at, size):
        part = scale[at : at + size, :]
        return jnp.concatenate([part] * (width // 128), axis=1)

    for g in range(groups):
        at = g * ent_dev
        proj = dot(gathered[g, 0:ent_dev, :], theta[...])
        part = (es(at, ent_dev) * proj).astype(BF)
        values[at : at + ent_dev, :] = part
        values[ents + at : ents + at + ent_dev, :] = part
    for g in range(groups):
        at = g * ent_dev
        preact = es(at, ent_dev) * dot(full[at : at + ent_dev, :], values[...])
        gate = jax.nn.sigmoid(preact)
        acts[at : at + ent_dev, :] = (preact * gate).astype(BF)
        cot = gathered[g, ent_dev:, :].astype(F32)
        grad = cot * gate * (1.0 + preact * (1.0 - gate))
        part = (es(at, ent_dev) * grad).astype(BF)
        backs[at : at + ent_dev, :] = part
        backs[ents + at : ents + at + ent_dev, :] = part
    own_rows = pl.ds(pl.multiple_of(mine * ent_dev, ent_dev), ent_dev)
    activated[...] = acts[own_rows, :]
    total = jnp.zeros((width, width), F32)
    for g in range(groups):
        at = g * ent_dev
        part = (es(at, ent_dev) * dot(full[at : at + ent_dev, :], backs[...])).astype(BF)
        projs[at : at + ent_dev, :] = part
        total = total + dot(gathered[g, 0:ent_dev, :], part, TN)
    grad_theta[...] = total
    grad_features[...] = dot(projs[own_rows, :], theta[...], NT).astype(BF)
    sections = incidence.shape[0]
    for q in range(sections // 128):
        piece = incidence[q * 128 : (q + 1) * 128, :]
        ahead = dot(piece, values[0:ents, :])
        back = dot(piece, backs[0:ents, :])
        sums = column_to_row(jnp.sum(ahead * back, axis=1, keepdims=True))
        lanes = slice(q * 128, (q + 1) * 128)
        grad_weight[:, lanes] = sums * inverse[:, lanes]


def dense_body(features, theta, section_weight, pair_rows, pair_cols, pair_counts, cotangent):
    ent_dev, width = features.shape
    sec_dev = section_weight.shape[0]
    _, blocks, slots = pair_rows.shape
    ents = blocks * ent_dev
    tiles = ents // TILE
    chips = lax.axis_size("ent") * lax.axis_size("x")
    gathered = lax.all_gather(
        jnp.concatenate([features, cotangent], axis=0), "ent", axis=0, tiled=False
    )
    with jax.named_scope("lists"):
        payload, incidence, inverse = pl.pallas_call(
            prep_kernel,
            out_shape=(
                jax.ShapeDtypeStruct((chips, 3 * blocks, slots), BF),
                jax.ShapeDtypeStruct((sec_dev, ents), BF),
                jax.ShapeDtypeStruct((1, sec_dev), F32),
            ),
            in_specs=[pl.BlockSpec(memory_space=pltpu.SMEM), vmem(), vmem(), vmem()],
            out_specs=(vmem(), vmem(), vmem()),
            compiler_params=params(),
        )(pair_counts, pair_rows, pair_cols, section_weight.reshape(1, sec_dev))
        lists = lax.all_to_all(payload, ("ent", "x"), 0, 0, tiled=True)
    with jax.named_scope("gram"):
        heights = [ents - b * TILE for b in range(tiles)]
        gram_rows = sum(heights) + 16
        own = pl.pallas_call(
            gram_kernel,
            out_shape=jax.ShapeDtypeStruct((gram_rows, TILE), BF),
            in_specs=[vmem()],
            out_specs=vmem(),
            scratch_shapes=[
                pltpu.VMEM((ents, sec_dev), BF),
                pltpu.VMEM((ents + 16, sec_dev), BF),
            ]
            + [pltpu.VMEM((h + 16, TILE), F32) for h in heights],
            compiler_params=params(),
        )(lists)
        other = lax.ppermute(own, "core", [(0, 1), (1, 0)])
    with jax.named_scope("tail"):
        activated, grad_features, grad_theta, grad_weight = pl.pallas_call(
            tail_kernel,
            out_shape=(
                jax.ShapeDtypeStruct((ent_dev, width), BF),
                jax.ShapeDtypeStruct((ent_dev, width), BF),
                jax.ShapeDtypeStruct((width, width), F32),
                jax.ShapeDtypeStruct((1, sec_dev), F32),
            ),
            in_specs=[vmem()] * 6,
            out_specs=(vmem(),) * 4,
            scratch_shapes=[
                pltpu.VMEM((ents, 2 * ents), BF),
                pltpu.VMEM((ents, 128), F32),
                pltpu.VMEM((2 * ents, width), BF),
                pltpu.VMEM((2 * ents, width), BF),
                pltpu.VMEM((ents, width), BF),
                pltpu.VMEM((ents, width), BF),
            ],
            compiler_params=params(),
        )(own, other, gathered, theta, incidence, inverse)
    return activated, grad_features, grad_theta, grad_weight.reshape(sec_dev)


def solution(mesh):
    ent, sec = mesh.shape["ent"], mesh.shape["sec"]
    cores = 2
    dense = ent <= 8 and sec % cores == 0
    if dense:
        grid = Mesh(mesh.devices.reshape(ent, sec // cores, cores), ("ent", "x", "core"))
        split = ("ent", "x", "core")
    else:
        grid = mesh
        split = ("ent", "sec")
    placed = (
        P("ent", None),
        P(),
        P(split),
        P(split, None, None),
        P(split, None, None),
        P(split, None),
        P("ent", None),
    )
    return jax.shard_map(
        dense_body if dense else body,
        mesh=grid,
        in_specs=placed,
        out_specs=(P("ent", None), P("ent", None), P(), P(split)),
        check_vma=False,
    )
```

```python
import jax
import jax.numpy as jnp
from jax import lax
from jax.experimental import pallas as pl
from jax.experimental.pallas import tpu as pltpu
from jax.sharding import Mesh, PartitionSpec as P


def hot_table(indices, live_slots, offset, table_width):
    hits = (indices - offset)[:, None] == jnp.arange(table_width, dtype=jnp.int32)[None, :]
    return (hits & live_slots[:, None]).astype(jnp.bfloat16)


def body(features, theta, section_weight, pair_rows, pair_cols, pair_counts, cotangent):
    ent_dev = features.shape[0]
    feature_width = features.shape[1]
    sec_dev = section_weight.shape[0]
    blocks_count = pair_rows.shape[1]
    slot_count = pair_rows.shape[2]
    own_block = lax.axis_index("ent")
    row_lists = pair_rows[0]
    col_lists = pair_cols[0]
    usable = jnp.arange(slot_count, dtype=jnp.int32)[None, :] < pair_counts[0][:, None]
    usable_float = usable.astype(jnp.float32)
    entity_index = jnp.arange(blocks_count, dtype=jnp.int32)[:, None] * ent_dev + col_lists
    local_degree = jax.ops.segment_sum(
        usable_float.reshape(-1), entity_index.reshape(-1), num_segments=blocks_count * ent_dev
    )
    entity_degree = lax.psum(local_degree, ("ent", "sec"))
    own_degree = lax.dynamic_slice_in_dim(entity_degree, own_block * ent_dev, ent_dev)
    entity_scale = lax.rsqrt(1.0 + own_degree)[:, None]
    sec_count = jax.ops.segment_sum(
        usable_float.reshape(-1), row_lists.reshape(-1), num_segments=sec_dev
    )
    section_scale = (section_weight / (1.0 + sec_count))[:, None]

    def entity_fold(running, incoming, start_row):
        row_count = incoming.shape[0]
        span_width = min(row_count, ent_dev)
        block_span = max(row_count // ent_dev, 1)
        offset = start_row

        def add_block(turn_index, accum):
            row_slots = lax.dynamic_index_in_dim(row_lists, turn_index, 0, keepdims=False)
            col_slots = lax.dynamic_index_in_dim(col_lists, turn_index, 0, keepdims=False)
            live_slots = lax.dynamic_index_in_dim(usable, turn_index, 0, keepdims=False)
            values = lax.dynamic_slice_in_dim(incoming, turn_index * span_width, span_width, 0)
            col_hot = hot_table(col_slots, live_slots, offset, span_width)
            row_hot = hot_table(row_slots, live_slots, 0, sec_dev)
            picked = jnp.dot(col_hot, values, preferred_element_type=jnp.float32).astype(
                jnp.bfloat16
            )
            return accum + jnp.einsum(
                "ps,pf->sf", row_hot, picked, preferred_element_type=jnp.float32
            )

        return lax.fori_loop(0, block_span, add_block, running)

    def entity_terms(messages, start_row):
        span_width = min(lax.axis_size("ent") * ent_dev, ent_dev)
        block_span = max(lax.axis_size("ent") * ent_dev // ent_dev, 1)
        offset = start_row

        def block_term(turn_index):
            row_slots = lax.dynamic_index_in_dim(row_lists, turn_index, 0, keepdims=False)
            col_slots = lax.dynamic_index_in_dim(col_lists, turn_index, 0, keepdims=False)
            live_slots = lax.dynamic_index_in_dim(usable, turn_index, 0, keepdims=False)
            row_hot = hot_table(row_slots, live_slots, 0, sec_dev)
            col_hot = hot_table(col_slots, live_slots, offset, span_width)
            picked = jnp.dot(row_hot, messages, preferred_element_type=jnp.float32).astype(
                jnp.bfloat16
            )
            return jnp.einsum("pw,pf->wf", col_hot, picked, preferred_element_type=jnp.float32)

        pieces = lax.map(block_term, jnp.arange(block_span, dtype=jnp.int32))
        return pieces.reshape(block_span * span_width, feature_width)

    def collect(messages):
        partial_sum = lax.psum_scatter(
            entity_terms(messages, jnp.int32(0)), "ent", scatter_dimension=0, tiled=True
        )
        return lax.psum(partial_sum, "sec")

    zero_sections = jnp.zeros((sec_dev, feature_width), jnp.float32)
    projected = jnp.dot(features, theta, preferred_element_type=jnp.float32)
    scaled = (entity_scale * projected).astype(jnp.bfloat16)
    gathered = entity_fold(
        zero_sections, lax.all_gather(scaled, "ent", axis=0, tiled=True), jnp.int32(0)
    )
    messages = (section_scale * gathered).astype(jnp.bfloat16)
    collected = collect(messages)
    preact = entity_scale * collected
    activated = jax.nn.silu(preact).astype(jnp.bfloat16)
    sigmoid_pre = jax.nn.sigmoid(preact)
    grad_pre = cotangent.astype(jnp.float32) * sigmoid_pre * (1.0 + preact * (1.0 - sigmoid_pre))
    back_scaled = (entity_scale * grad_pre).astype(jnp.bfloat16)
    back_gathered = entity_fold(
        zero_sections, lax.all_gather(back_scaled, "ent", axis=0, tiled=True), jnp.int32(0)
    )
    grad_weight = jnp.sum(gathered * back_gathered, axis=1) / (1.0 + sec_count)
    back_messages = (section_scale * back_gathered).astype(jnp.bfloat16)
    back_collected = collect(back_messages)
    grad_proj = (entity_scale * back_collected).astype(jnp.bfloat16)
    grad_features = lax.dot_general(
        grad_proj, theta, (((1,), (1,)), ((), ())), preferred_element_type=jnp.float32
    ).astype(jnp.bfloat16)
    local_theta = lax.dot_general(
        features, grad_proj, (((0,), (0,)), ((), ())), preferred_element_type=jnp.float32
    )
    grad_theta = lax.psum(local_theta, "ent")
    return (activated, grad_features, grad_theta, grad_weight)


BF = jnp.bfloat16
F32 = jnp.float32
BIT = jnp.float8_e4m3fn
TILE = 256
SHIFT = TILE.bit_length() - 1
NT = (((1,), (1,)), ((), ()))
TN = (((0,), (0,)), ((), ()))
CORES = 2
STEP = 4


def params(mebibytes=32):
    return pltpu.CompilerParams(vmem_limit_bytes=mebibytes * 2**20)


def vmem():
    return pl.BlockSpec(memory_space=pltpu.VMEM)


def hbm():
    return pl.BlockSpec(memory_space=pltpu.HBM)


def dot(a, b, dims=(((1,), (0,)), ((), ()))):
    return lax.dot_general(a, b, dims, preferred_element_type=F32)


def one_hot(index_row, count=TILE):
    ids = lax.broadcasted_iota(jnp.int32, (count, index_row.shape[1]), 0).astype(BF)
    return jnp.where(ids == index_row, jnp.ones((), BIT), jnp.zeros((), BIT))


def column_to_row(column):
    wide = jnp.broadcast_to(column, (column.shape[0], 128))
    return wide.T[0:1, :]


def row_to_column(row):
    return jnp.broadcast_to(row, (128, 128)).T


def prep_kernel(
    counts, rows, cols, weight, features, cotangent,
    payload, shares, message, inverse,
    counts_here, rows_here, cols_here, weight_here, share_here, in_sems, out_sems, share_sems,
):
    copies, height, slots = payload.shape
    blocks = rows.shape[1]
    ent_dev = features.shape[0]
    share = shares.shape[1] // 2
    quarter = lax.axis_index("x") * CORES + lax.axis_index("core")
    here = pl.ds(pl.multiple_of(quarter * share, share), share)
    reads = [
        pltpu.make_async_copy(source, target, in_sems.at[n])
        for n, (source, target) in enumerate(
            (
                (counts, counts_here),
                (rows.at[0], rows_here),
                (cols.at[0], cols_here),
                (weight, weight_here),
                (features.at[here, :], share_here.at[0:share, :]),
                (cotangent.at[here, :], share_here.at[share : 2 * share, :]),
            )
        )
    ]
    for read in reads:
        read.start()
    for read in reads:
        read.wait()
    sends = [
        pltpu.make_async_copy(share_here, shares.at[n], share_sems.at[n]) for n in range(copies)
    ]
    for send in sends:
        send.start()
    row_ids = rows_here[...]
    sub = lax.broadcasted_iota(jnp.int32, (blocks, slots), 0)
    lane = lax.broadcasted_iota(jnp.int32, (blocks, slots), 1)
    limit = jnp.zeros((blocks, slots), jnp.int32)
    for j in range(blocks):
        limit = jnp.where(sub == j, counts_here[0, j], limit)
    live = lane < limit
    part = lax.shift_right_logical(row_ids, SHIFT)
    high = jnp.where(live, part * ent_dev + cols_here[...], -1).astype(F32)
    low = jnp.where(live, row_ids & (TILE - 1), -1).astype(F32)
    part = part.astype(F32)
    degree = jnp.zeros((16, TILE), F32)
    for j in range(blocks):
        degree = degree + dot(
            one_hot(part[j : j + 1].astype(BF), 16), one_hot(low[j : j + 1].astype(BF)), NT
        )
    degree = jnp.concatenate([degree[0:1], degree[1:2]], axis=1)
    inverse[...] = 1.0 / (1.0 + degree)
    scale = weight_here[...] / (1.0 + degree)
    message[...] = jnp.concatenate(
        [high, low, jnp.broadcast_to(scale, (height - 2 * blocks, slots))], axis=0
    ).astype(BF)
    writes = [
        pltpu.make_async_copy(message, payload.at[n], out_sems.at[n]) for n in range(copies)
    ]
    for write in writes:
        write.start()
    for write in writes + sends:
        write.wait()


def own_kernel(message, incidence):
    blocks = message.shape[0] // 3
    ent_dev = incidence.shape[1] // blocks
    for j in range(blocks):
        block = dot(
            one_hot(message[blocks + j : blocks + j + 1, :]), one_hot(message[j : j + 1, :]), NT
        ).astype(BF)
        for half in range(2):
            incidence[half * TILE : (half + 1) * TILE, j * ent_dev : (j + 1) * ent_dev] = block[
                :, half * ent_dev : (half + 1) * ent_dev
            ]


def gram_kernel(lists, gram, table, scaled, *sums):
    shards, height, slots = lists.shape
    ents = table.shape[0]
    blocks = height // 3
    ent_dev = ents // blocks
    tiles = ents // TILE
    sections = table.shape[1] // STEP
    for acc in sums:
        acc[...] = jnp.zeros_like(acc)
    scaled[ents:, :] = jnp.ones((scaled.shape[0] - ents, scaled.shape[1]), BF)

    def step(i, carry):
        for q in range(STEP):
            indices = lists[i * STEP + q]
            scale = indices[2 * blocks : 2 * blocks + 1]
            for j in range(blocks):
                block = dot(
                    one_hot(indices[j : j + 1]), one_hot(indices[blocks + j : blocks + j + 1]), NT
                ).astype(BF)
                rows = slice(j * ent_dev, (j + 1) * ent_dev)
                for half in range(2):
                    at = q * sections + half * TILE
                    part = block[half * ent_dev : (half + 1) * ent_dev, :]
                    table[rows, at : at + TILE] = part
                    scaled[rows, at : at + TILE] = part * scale[:, half * TILE : (half + 1) * TILE]
        for b in range(tiles):
            sums[b][...] += dot(scaled[b * TILE :, :], table[b * TILE : (b + 1) * TILE, :], NT)
        return carry

    lax.fori_loop(0, shards // STEP, step, 0)
    start = 0
    degrees = []
    for b in range(tiles):
        size = ents - b * TILE
        gram[start : start + size, :] = sums[b][0:size, :].astype(BF)
        start += size
        degree = sums[b][size : size + 1, :]
        top = degree.astype(BF).astype(F32)
        degrees += [top, degree - top]
    degrees.append(jnp.zeros((16 - 2 * tiles, TILE), F32))
    gram[start : start + 16, :] = jnp.concatenate(degrees, axis=0).astype(BF)


def tail_kernel(
    own, other, own_share, other_share, theta, incidence, inverse,
    activated, grad_features, grad_theta, grad_weight,
    full, scale, values, backs, acts, projs, feats, cots, sems,
):
    ents = full.shape[0]
    tiles = ents // TILE
    ent_dev = activated.shape[0]
    groups = ents // ent_dev
    width = theta.shape[0]
    share = feats.shape[2]
    per_group = feats.shape[0] // groups
    core = lax.axis_index("core")
    mine = lax.axis_index("ent")
    loads = []
    for n, source in enumerate((own_share, other_share)):
        at = core if n == 0 else 1 - core
        loads.append(pltpu.make_async_copy(source.at[:, 0:share, :], feats.at[:, at], sems.at[2 * n]))
        loads.append(
            pltpu.make_async_copy(source.at[:, share : 2 * share, :], cots.at[:, at], sems.at[2 * n + 1])
        )
    for load in loads:
        load.start()
    base = sum(ents - b * TILE for b in range(tiles))
    degree_rows = own[base : base + 16, :].astype(F32) + other[base : base + 16, :].astype(F32)
    for b in range(tiles):
        row = lax.rsqrt(1.0 + (degree_rows[2 * b : 2 * b + 1] + degree_rows[2 * b + 1 : 2 * b + 2]))
        for h in range(TILE // 128):
            at = b * TILE + h * 128
            scale[at : at + 128, :] = row_to_column(row[:, h * 128 : (h + 1) * 128])
    for n, source in enumerate((own, other)):
        column = (core if n == 0 else 1 - core) * ents
        start = 0
        for b in range(tiles):
            for a in range(b, tiles):
                piece = source[start : start + TILE, :]
                full[a * TILE : (a + 1) * TILE, pl.ds(pl.multiple_of(column + b * TILE, TILE), TILE)] = piece
                if a != b:
                    full[b * TILE : (b + 1) * TILE, pl.ds(pl.multiple_of(column + a * TILE, TILE), TILE)] = piece.T
                start += TILE
    for load in loads:
        load.wait()

    def es(at, size):
        part = scale[at : at + size, :]
        return jnp.concatenate([part] * (width // 128), axis=1)

    def rows_of(stack, g):
        return stack[g * per_group : (g + 1) * per_group].reshape(ent_dev, width)

    for g in range(groups):
        at = g * ent_dev
        proj = dot(rows_of(feats, g), theta[...])
        part = (es(at, ent_dev) * proj).astype(BF)
        values[at : at + ent_dev, :] = part
        values[ents + at : ents + at + ent_dev, :] = part
    for g in range(groups):
        at = g * ent_dev
        preact = es(at, ent_dev) * dot(full[at : at + ent_dev, :], values[...])
        gate = jax.nn.sigmoid(preact)
        acts[at : at + ent_dev, :] = (preact * gate).astype(BF)
        grad = rows_of(cots, g).astype(F32) * gate * (1.0 + preact * (1.0 - gate))
        part = (es(at, ent_dev) * grad).astype(BF)
        backs[at : at + ent_dev, :] = part
        backs[ents + at : ents + at + ent_dev, :] = part
    own_rows = pl.ds(pl.multiple_of(mine * ent_dev, ent_dev), ent_dev)
    activated[...] = acts[own_rows, :]
    total = jnp.zeros((width, width), F32)
    for g in range(groups):
        at = g * ent_dev
        part = (es(at, ent_dev) * dot(full[at : at + ent_dev, :], backs[...])).astype(BF)
        projs[at : at + ent_dev, :] = part
        total = total + dot(rows_of(feats, g), part, TN)
    grad_theta[...] = total
    grad_features[...] = dot(projs[own_rows, :], theta[...], NT).astype(BF)
    sections = incidence.shape[0]
    for q in range(sections // 128):
        piece = incidence[q * 128 : (q + 1) * 128, :]
        ahead = dot(piece, values[0:ents, :])
        back = dot(piece, backs[0:ents, :])
        sums = column_to_row(jnp.sum(ahead * back, axis=1, keepdims=True))
        lanes = slice(q * 128, (q + 1) * 128)
        grad_weight[:, lanes] = sums * inverse[:, lanes]


def dense_body(features, theta, section_weight, pair_rows, pair_cols, pair_counts, cotangent):
    ent_dev, width = features.shape
    sec_dev = section_weight.shape[0]
    _, blocks, slots = pair_rows.shape
    ents = blocks * ent_dev
    tiles = ents // TILE
    lanes = lax.axis_size("x")
    chips = lax.axis_size("ent") * lanes
    share = ent_dev // (lanes * CORES)
    height = 3 * blocks
    dma = pltpu.SemaphoreType.DMA
    swap = [(0, 1), (1, 0)]
    payload, shares, message, inverse = pl.pallas_call(
        prep_kernel,
        out_shape=(
            jax.ShapeDtypeStruct((chips, height, slots), BF),
            jax.ShapeDtypeStruct((chips, 2 * share, width), BF),
            jax.ShapeDtypeStruct((height, slots), BF),
            jax.ShapeDtypeStruct((1, sec_dev), F32),
        ),
        in_specs=[hbm()] * 6,
        out_specs=(hbm(), hbm(), vmem(), vmem()),
        scratch_shapes=[
            pltpu.SMEM((1, blocks), jnp.int32),
            pltpu.VMEM((blocks, slots), jnp.int32),
            pltpu.VMEM((blocks, slots), jnp.int32),
            pltpu.VMEM((1, sec_dev), F32),
            pltpu.VMEM((2 * share, width), BF),
            dma((6,)),
            dma((chips,)),
            dma((chips,)),
        ],
        compiler_params=params(63),
        name="prep",
    )(pair_counts, pair_rows, pair_cols, section_weight.reshape(1, sec_dev), features, cotangent)
    lists = lax.all_to_all(payload, ("ent", "x"), 0, 0, tiled=True)
    incidence = pl.pallas_call(
        own_kernel,
        out_shape=jax.ShapeDtypeStruct((sec_dev, ents), BF),
        in_specs=[vmem()],
        out_specs=vmem(),
        compiler_params=params(),
        cost_estimate=pl.CostEstimate(flops=2 * sec_dev * ents * slots, bytes_accessed=2**20, transcendentals=0),
        name="own_incidence",
    )(message)
    lists, shares = lax.optimization_barrier((lists, shares))
    own_share = lax.all_to_all(shares, ("ent", "x"), 0, 0, tiled=True)
    heights = [ents - b * TILE for b in range(tiles)]
    own = pl.pallas_call(
        gram_kernel,
        out_shape=jax.ShapeDtypeStruct((sum(heights) + 16, TILE), BF),
        in_specs=[vmem()],
        out_specs=vmem(),
        scratch_shapes=[
            pltpu.VMEM((ents, STEP * sec_dev), BF),
            pltpu.VMEM((ents + 16, STEP * sec_dev), BF),
        ]
        + [pltpu.VMEM((h + 16, TILE), F32) for h in heights],
        compiler_params=params(),
        cost_estimate=pl.CostEstimate(
            flops=2 * chips * sec_dev * (sum(heights) * TILE + ents * slots), bytes_accessed=2**21, transcendentals=0
        ),
        name="gram",
    )(lists)
    other = lax.ppermute(own, "core", swap)
    other_share = lax.ppermute(own_share, "core", swap)
    activated, grad_features, grad_theta, grad_weight = pl.pallas_call(
        tail_kernel,
        out_shape=(
            jax.ShapeDtypeStruct((ent_dev, width), BF),
            jax.ShapeDtypeStruct((ent_dev, width), BF),
            jax.ShapeDtypeStruct((width, width), F32),
            jax.ShapeDtypeStruct((1, sec_dev), F32),
        ),
        in_specs=[vmem(), vmem(), hbm(), hbm(), vmem(), vmem(), vmem()],
        out_specs=(vmem(),) * 4,
        scratch_shapes=[
            pltpu.VMEM((ents, 2 * ents), BF),
            pltpu.VMEM((ents, 128), F32),
            pltpu.VMEM((2 * ents, width), BF),
            pltpu.VMEM((2 * ents, width), BF),
            pltpu.VMEM((ents, width), BF),
            pltpu.VMEM((ents, width), BF),
            pltpu.VMEM((chips, CORES, share, width), BF),
            pltpu.VMEM((chips, CORES, share, width), BF),
            dma((4,)),
        ],
        compiler_params=params(),
        name="tail",
    )(own, other, own_share, other_share, theta, incidence, inverse)
    return activated, grad_features, grad_theta, grad_weight.reshape(sec_dev)


def solution(mesh):
    ent, sec = mesh.shape["ent"], mesh.shape["sec"]
    dense = ent <= 8 and sec % CORES == 0
    if dense:
        grid = Mesh(mesh.devices.reshape(ent, sec // CORES, CORES), ("ent", "x", "core"))
        split = ("ent", "x", "core")
    else:
        grid = mesh
        split = ("ent", "sec")
    placed = (
        P("ent", None),
        P(),
        P(split),
        P(split, None, None),
        P(split, None, None),
        P(split, None),
        P("ent", None),
    )
    return jax.shard_map(
        dense_body if dense else body,
        mesh=grid,
        in_specs=placed,
        out_specs=(P("ent", None), P("ent", None), P(), P(split)),
        check_vma=False,
    )
```

```python
import jax
import jax.numpy as jnp
from jax import lax
from jax.experimental import pallas as pl
from jax.experimental.pallas import tpu as pltpu
from jax.sharding import Mesh, PartitionSpec as P


def hot_table(indices, live_slots, offset, table_width):
    hits = (indices - offset)[:, None] == jnp.arange(table_width, dtype=jnp.int32)[None, :]
    return (hits & live_slots[:, None]).astype(jnp.bfloat16)


def body(features, theta, section_weight, pair_rows, pair_cols, pair_counts, cotangent):
    ent_dev = features.shape[0]
    feature_width = features.shape[1]
    sec_dev = section_weight.shape[0]
    blocks_count = pair_rows.shape[1]
    slot_count = pair_rows.shape[2]
    own_block = lax.axis_index("ent")
    row_lists = pair_rows[0]
    col_lists = pair_cols[0]
    usable = jnp.arange(slot_count, dtype=jnp.int32)[None, :] < pair_counts[0][:, None]
    usable_float = usable.astype(jnp.float32)
    entity_index = jnp.arange(blocks_count, dtype=jnp.int32)[:, None] * ent_dev + col_lists
    local_degree = jax.ops.segment_sum(
        usable_float.reshape(-1), entity_index.reshape(-1), num_segments=blocks_count * ent_dev
    )
    entity_degree = lax.psum(local_degree, ("ent", "sec"))
    own_degree = lax.dynamic_slice_in_dim(entity_degree, own_block * ent_dev, ent_dev)
    entity_scale = lax.rsqrt(1.0 + own_degree)[:, None]
    sec_count = jax.ops.segment_sum(
        usable_float.reshape(-1), row_lists.reshape(-1), num_segments=sec_dev
    )
    section_scale = (section_weight / (1.0 + sec_count))[:, None]

    def entity_fold(running, incoming, start_row):
        row_count = incoming.shape[0]
        span_width = min(row_count, ent_dev)
        block_span = max(row_count // ent_dev, 1)
        offset = start_row

        def add_block(turn_index, accum):
            row_slots = lax.dynamic_index_in_dim(row_lists, turn_index, 0, keepdims=False)
            col_slots = lax.dynamic_index_in_dim(col_lists, turn_index, 0, keepdims=False)
            live_slots = lax.dynamic_index_in_dim(usable, turn_index, 0, keepdims=False)
            values = lax.dynamic_slice_in_dim(incoming, turn_index * span_width, span_width, 0)
            col_hot = hot_table(col_slots, live_slots, offset, span_width)
            row_hot = hot_table(row_slots, live_slots, 0, sec_dev)
            picked = jnp.dot(col_hot, values, preferred_element_type=jnp.float32).astype(
                jnp.bfloat16
            )
            return accum + jnp.einsum(
                "ps,pf->sf", row_hot, picked, preferred_element_type=jnp.float32
            )

        return lax.fori_loop(0, block_span, add_block, running)

    def entity_terms(messages, start_row):
        span_width = min(lax.axis_size("ent") * ent_dev, ent_dev)
        block_span = max(lax.axis_size("ent") * ent_dev // ent_dev, 1)
        offset = start_row

        def block_term(turn_index):
            row_slots = lax.dynamic_index_in_dim(row_lists, turn_index, 0, keepdims=False)
            col_slots = lax.dynamic_index_in_dim(col_lists, turn_index, 0, keepdims=False)
            live_slots = lax.dynamic_index_in_dim(usable, turn_index, 0, keepdims=False)
            row_hot = hot_table(row_slots, live_slots, 0, sec_dev)
            col_hot = hot_table(col_slots, live_slots, offset, span_width)
            picked = jnp.dot(row_hot, messages, preferred_element_type=jnp.float32).astype(
                jnp.bfloat16
            )
            return jnp.einsum("pw,pf->wf", col_hot, picked, preferred_element_type=jnp.float32)

        pieces = lax.map(block_term, jnp.arange(block_span, dtype=jnp.int32))
        return pieces.reshape(block_span * span_width, feature_width)

    def collect(messages):
        partial_sum = lax.psum_scatter(
            entity_terms(messages, jnp.int32(0)), "ent", scatter_dimension=0, tiled=True
        )
        return lax.psum(partial_sum, "sec")

    zero_sections = jnp.zeros((sec_dev, feature_width), jnp.float32)
    projected = jnp.dot(features, theta, preferred_element_type=jnp.float32)
    scaled = (entity_scale * projected).astype(jnp.bfloat16)
    gathered = entity_fold(
        zero_sections, lax.all_gather(scaled, "ent", axis=0, tiled=True), jnp.int32(0)
    )
    messages = (section_scale * gathered).astype(jnp.bfloat16)
    collected = collect(messages)
    preact = entity_scale * collected
    activated = jax.nn.silu(preact).astype(jnp.bfloat16)
    sigmoid_pre = jax.nn.sigmoid(preact)
    grad_pre = cotangent.astype(jnp.float32) * sigmoid_pre * (1.0 + preact * (1.0 - sigmoid_pre))
    back_scaled = (entity_scale * grad_pre).astype(jnp.bfloat16)
    back_gathered = entity_fold(
        zero_sections, lax.all_gather(back_scaled, "ent", axis=0, tiled=True), jnp.int32(0)
    )
    grad_weight = jnp.sum(gathered * back_gathered, axis=1) / (1.0 + sec_count)
    back_messages = (section_scale * back_gathered).astype(jnp.bfloat16)
    back_collected = collect(back_messages)
    grad_proj = (entity_scale * back_collected).astype(jnp.bfloat16)
    grad_features = lax.dot_general(
        grad_proj, theta, (((1,), (1,)), ((), ())), preferred_element_type=jnp.float32
    ).astype(jnp.bfloat16)
    local_theta = lax.dot_general(
        features, grad_proj, (((0,), (0,)), ((), ())), preferred_element_type=jnp.float32
    )
    grad_theta = lax.psum(local_theta, "ent")
    return (activated, grad_features, grad_theta, grad_weight)


BF = jnp.bfloat16
F32 = jnp.float32
BIT = jnp.float8_e4m3fn
TILE = 256
SHIFT = TILE.bit_length() - 1
NT = (((1,), (1,)), ((), ()))
TN = (((0,), (0,)), ((), ()))
CORES = 2
CHUNKS = 4


def params(mebibytes=32):
    return pltpu.CompilerParams(vmem_limit_bytes=mebibytes * 2**20)


def vmem():
    return pl.BlockSpec(memory_space=pltpu.VMEM)


def hbm():
    return pl.BlockSpec(memory_space=pltpu.HBM)


def dot(a, b, dims=(((1,), (0,)), ((), ()))):
    return lax.dot_general(a, b, dims, preferred_element_type=F32)


def one_hot(index_row, count=TILE):
    ids = lax.broadcasted_iota(jnp.int32, (count, index_row.shape[1]), 0).astype(BF)
    return jnp.where(ids == index_row, jnp.ones((), BIT), jnp.zeros((), BIT))


def index_hot(lists, j, chunks):
    parts = [one_hot(lists[16 * c + j : 16 * c + j + 1, :]) for c in range(chunks)]
    return jnp.concatenate(parts, axis=1)


def column_to_row(column):
    wide = jnp.broadcast_to(column, (column.shape[0], 128))
    return wide.T[0:1, :]


def row_to_column(row):
    return jnp.broadcast_to(row, (128, 128)).T


def prep_kernel(
    counts, rows, cols, weight, features, cotangent, payload, shares, inverse,
    counts_here, rows_here, cols_here, weight_here, share_here, sems, share_sems,
):
    _, blocks, slots = rows.shape
    chunks = slots // 128
    ent_dev = features.shape[0]
    share = share_here.shape[0] // 2
    quarter = lax.axis_index("x") * CORES + lax.axis_index("core")
    here = pl.ds(pl.multiple_of(quarter * share, share), share)
    reads = [
        pltpu.make_async_copy(source, target, sems.at[n])
        for n, (source, target) in enumerate(
            (
                (counts, counts_here),
                (rows.at[0], rows_here),
                (cols.at[0], cols_here),
                (weight, weight_here),
                (features.at[here, :], share_here.at[0:share, :]),
                (cotangent.at[here, :], share_here.at[share : 2 * share, :]),
            )
        )
    ]
    for read in reads:
        read.start()
    for read in reads:
        read.wait()
    sends = [
        pltpu.make_async_copy(share_here, shares.at[n], share_sems.at[n])
        for n in range(shares.shape[0])
    ]
    for send in sends:
        send.start()
    row_ids = rows_here[...]
    sub = lax.broadcasted_iota(jnp.int32, (blocks, slots), 0)
    lane = lax.broadcasted_iota(jnp.int32, (blocks, slots), 1)
    limit = jnp.zeros((blocks, slots), jnp.int32)
    for j in range(blocks):
        limit = jnp.where(sub == j, counts_here[0, j], limit)
    live = lane < limit
    part = lax.shift_right_logical(row_ids, SHIFT)
    high = jnp.where(live, part * ent_dev + cols_here[...], -1).astype(F32)
    low = jnp.where(live, row_ids & (TILE - 1), -1).astype(F32)
    part = part.astype(F32)
    degree = jnp.zeros((16, TILE), F32)
    for j in range(blocks):
        degree = degree + dot(
            one_hot(part[j : j + 1].astype(BF), 16), one_hot(low[j : j + 1].astype(BF)), NT
        )
    degree = jnp.concatenate([degree[0:1], degree[1:2]], axis=1)
    inverse[...] = 1.0 / (1.0 + degree)
    scale = weight_here[...] / (1.0 + degree)
    indices = jnp.concatenate([high, low], axis=0).astype(BF)
    for c in range(chunks):
        payload[16 * c : 16 * (c + 1), :] = indices[:, 128 * c : 128 * (c + 1)]
    ends = [scale[:, 128 * c : 128 * (c + 1)] for c in range(chunks)]
    ends.append(jnp.zeros((8 - chunks, 128), F32))
    at = 16 * chunks
    payload[at : at + 8, :] = jnp.concatenate(ends, axis=0).astype(BF)
    for send in sends:
        send.wait()


def hold_kernel(source, target):
    target[...] = source[...]


def own_kernel(payload, incidence):
    ents = incidence.shape[1]
    ent_dev = TILE // (incidence.shape[0] // TILE)
    chunks = CHUNKS
    for j in range(ents // ent_dev):
        block = dot(index_hot(payload, 8 + j, chunks), index_hot(payload, j, chunks), NT).astype(BF)
        for half in range(2):
            incidence[half * TILE : (half + 1) * TILE, j * ent_dev : (j + 1) * ent_dev] = block[
                :, half * ent_dev : (half + 1) * ent_dev
            ]


def collect_kernel(own, by_x, by_y, by_both, group):
    mine = lax.axis_index("y") * 2 + lax.axis_index("x")
    for d, source in enumerate((own, by_x, by_y, by_both)):
        group[jnp.bitwise_xor(mine, d)] = source[...]


def column_rows(ents):
    spans, start = [], 0
    for b in range(ents // TILE):
        end = start + ents - b * TILE + 16
        spans.append((start, end))
        start = end
    return spans


def fill(lists, table, scaled):
    shards = lists.shape[0]
    chunks = CHUNKS
    ents = table.shape[0]
    sections = table.shape[1] // shards
    ent_dev = TILE // (sections // TILE)
    scaled[ents:, :] = jnp.ones((scaled.shape[0] - ents, scaled.shape[1]), BF)
    for q in range(shards):
        indices = lists.at[q]
        scale = jnp.concatenate(
            [indices[16 * chunks + c : 16 * chunks + c + 1, :] for c in range(chunks)], axis=1
        )
        for j in range(ents // ent_dev):
            block = dot(index_hot(indices, j, chunks), index_hot(indices, 8 + j, chunks), NT).astype(BF)
            rows = slice(j * ent_dev, (j + 1) * ent_dev)
            for half in range(2):
                at = q * sections + half * TILE
                part = block[half * ent_dev : (half + 1) * ent_dev, :]
                table[rows, at : at + TILE] = part
                scaled[rows, at : at + TILE] = part * scale[:, half * TILE : (half + 1) * TILE]


def column(b, table, scaled):
    return dot(scaled[b * TILE :, :], table[b * TILE : (b + 1) * TILE, :], NT)


def first_kernel(lists, sums, table, scaled):
    fill(lists, table, scaled)
    for b, (start, end) in enumerate(column_rows(table.shape[0])):
        sums[start:end, :] = column(b, table, scaled)


def second_kernel(lists, before, sums, table, scaled):
    fill(lists, table, scaled)
    for b, (start, end) in enumerate(column_rows(table.shape[0])):
        sums[start:end, :] = before[start:end, :] + column(b, table, scaled)


def last_kernel(lists, pair, single, gram, table, scaled):
    ents = table.shape[0]
    spans = column_rows(ents)
    fill(lists, table, scaled)
    at = 0
    degrees = []
    for b, (start, end) in enumerate(spans):
        size = end - start - 16
        total = pair[start:end, :] + (single[start:end, :] + column(b, table, scaled))
        gram[at : at + size, :] = total[0:size].astype(BF)
        at += size
        degree = total[size : size + 1]
        top = degree.astype(BF).astype(F32)
        degrees += [top, degree - top]
    degrees.append(jnp.zeros((16 - 2 * len(spans), TILE), F32))
    gram[at : at + 16, :] = jnp.concatenate(degrees, axis=0).astype(BF)


def tail_kernel(
    own, other, own_share, other_share, theta, incidence, inverse,
    activated, grad_features, grad_theta, grad_weight,
    full, scale, values, backs, acts, projs, feats, cots,
):
    ents = full.shape[0]
    tiles = ents // TILE
    ent_dev = activated.shape[0]
    groups = ents // ent_dev
    width = theta.shape[0]
    share = feats.shape[2]
    per_group = feats.shape[0] // groups
    core = lax.axis_index("core")
    mine = lax.axis_index("z") * 2 + lax.axis_index("y")
    base = sum(ents - b * TILE for b in range(tiles))
    for n, source in enumerate((own_share, other_share)):
        which = core if n == 0 else 1 - core
        for q in range(source.shape[0]):
            feats[q, which] = source[q, 0:share, :]
            cots[q, which] = source[q, share : 2 * share, :]
    degree_rows = own[base : base + 16, :].astype(F32) + other[base : base + 16, :].astype(F32)
    for b in range(tiles):
        row = lax.rsqrt(1.0 + (degree_rows[2 * b : 2 * b + 1] + degree_rows[2 * b + 1 : 2 * b + 2]))
        for h in range(TILE // 128):
            at = b * TILE + h * 128
            scale[at : at + 128, :] = row_to_column(row[:, h * 128 : (h + 1) * 128])
    for n, source in enumerate((own, other)):
        column = (core if n == 0 else 1 - core) * ents
        start = 0
        for b in range(tiles):
            for a in range(b, tiles):
                piece = source[start : start + TILE, :]
                full[a * TILE : (a + 1) * TILE, pl.ds(pl.multiple_of(column + b * TILE, TILE), TILE)] = piece
                if a != b:
                    full[b * TILE : (b + 1) * TILE, pl.ds(pl.multiple_of(column + a * TILE, TILE), TILE)] = piece.T
                start += TILE

    def es(at, size):
        part = scale[at : at + size, :]
        return jnp.concatenate([part] * (width // 128), axis=1)

    def rows_of(stack, g):
        return stack[g * per_group : (g + 1) * per_group].reshape(ent_dev, width)

    for g in range(groups):
        at = g * ent_dev
        proj = dot(rows_of(feats, g), theta[...])
        part = (es(at, ent_dev) * proj).astype(BF)
        values[at : at + ent_dev, :] = part
        values[ents + at : ents + at + ent_dev, :] = part
    for g in range(groups):
        at = g * ent_dev
        preact = es(at, ent_dev) * dot(full[at : at + ent_dev, :], values[...])
        gate = jax.nn.sigmoid(preact)
        acts[at : at + ent_dev, :] = (preact * gate).astype(BF)
        grad = rows_of(cots, g).astype(F32) * gate * (1.0 + preact * (1.0 - gate))
        part = (es(at, ent_dev) * grad).astype(BF)
        backs[at : at + ent_dev, :] = part
        backs[ents + at : ents + at + ent_dev, :] = part
    own_rows = pl.ds(pl.multiple_of(mine * ent_dev, ent_dev), ent_dev)
    activated[...] = acts[own_rows, :]
    total = jnp.zeros((width, width), F32)
    for g in range(groups):
        at = g * ent_dev
        part = (es(at, ent_dev) * dot(full[at : at + ent_dev, :], backs[...])).astype(BF)
        projs[at : at + ent_dev, :] = part
        total = total + dot(rows_of(feats, g), part, TN)
    grad_theta[...] = total
    grad_features[...] = dot(projs[own_rows, :], theta[...], NT).astype(BF)
    sections = incidence.shape[0]
    for q in range(sections // 128):
        piece = incidence[q * 128 : (q + 1) * 128, :]
        ahead = dot(piece, values[0:ents, :])
        back = dot(piece, backs[0:ents, :])
        sums = column_to_row(jnp.sum(ahead * back, axis=1, keepdims=True))
        lanes = slice(q * 128, (q + 1) * 128)
        grad_weight[:, lanes] = sums * inverse[:, lanes]


def dense_body(features, theta, section_weight, pair_rows, pair_cols, pair_counts, cotangent):
    ent_dev, width = features.shape
    sec_dev = section_weight.shape[0]
    _, blocks, slots = pair_rows.shape
    ents = blocks * ent_dev
    tiles = ents // TILE
    group = lax.axis_size("y") * lax.axis_size("x")
    layers = lax.axis_size("z")
    share = ent_dev // (lax.axis_size("x") * CORES)
    height = CHUNKS * 16 + 8
    swap = [(0, 1), (1, 0)]
    payload, shares, inverse = pl.pallas_call(
        prep_kernel,
        out_shape=(
            jax.ShapeDtypeStruct((height, 128), BF),
            jax.ShapeDtypeStruct((layers * group, 2 * share, width), BF),
            jax.ShapeDtypeStruct((1, sec_dev), F32),
        ),
        in_specs=[hbm()] * 6,
        out_specs=(vmem(), hbm(), vmem()),
        scratch_shapes=[
            pltpu.SMEM((1, blocks), jnp.int32),
            pltpu.VMEM((blocks, slots), jnp.int32),
            pltpu.VMEM((blocks, slots), jnp.int32),
            pltpu.VMEM((1, sec_dev), F32),
            pltpu.VMEM((2 * share, width), BF),
            pltpu.SemaphoreType.DMA((6,)),
            pltpu.SemaphoreType.DMA((layers * group,)),
        ],
        compiler_params=params(63),
        name="prep",
    )(pair_counts, pair_rows, pair_cols, section_weight.reshape(1, sec_dev), features, cotangent)
    by_x = lax.ppermute(payload, "x", swap)
    by_y = lax.ppermute(payload, "y", swap)
    by_both = lax.ppermute(payload, ("y", "x"), [(i, i ^ 3) for i in range(4)])
    incidence = pl.pallas_call(
        own_kernel,
        out_shape=jax.ShapeDtypeStruct((sec_dev, ents), BF),
        in_specs=[vmem()],
        out_specs=vmem(),
        compiler_params=params(),
        cost_estimate=pl.CostEstimate(flops=2 * sec_dev * ents * slots, bytes_accessed=2**20, transcendentals=0),
        name="own_incidence",
    )(payload)
    held = pl.pallas_call(
        hold_kernel,
        out_shape=jax.ShapeDtypeStruct(payload.shape, BF),
        in_specs=[vmem()],
        out_specs=vmem(),
        compiler_params=params(),
        name="hold",
    )(payload)
    near = pl.pallas_call(
        collect_kernel,
        out_shape=jax.ShapeDtypeStruct((group,) + payload.shape, BF),
        in_specs=[vmem()] * 4,
        out_specs=vmem(),
        compiler_params=params(),
        name="collect",
    )(held, by_x, by_y, by_both)

    shares, near = lax.optimization_barrier((shares, near))

    def across(d):
        return lax.ppermute(near, "z", [(i, i ^ d) for i in range(layers)])

    far = [near] + [across(d) for d in range(1, layers)]
    rows = column_rows(ents)[-1][1]
    scratch = [pltpu.VMEM((ents, group * sec_dev), BF), pltpu.VMEM((ents + 16, group * sec_dev), BF)]

    def step(kernel, shape, kind, name, inputs):
        return pl.pallas_call(
            kernel,
            out_shape=jax.ShapeDtypeStruct(shape, kind),
            in_specs=jax.tree.map(lambda _: vmem(), list(inputs)),
            out_specs=vmem(),
            scratch_shapes=scratch,
            compiler_params=params(),
            cost_estimate=pl.CostEstimate(
                flops=1000000000, bytes_accessed=1000, transcendentals=0
            ),
            name=name,
        )(*inputs)

    sums = step(first_kernel, (rows, TILE), F32, "gram_first", [far[0]])
    pair = step(second_kernel, (rows, TILE), F32, "gram_second", [far[1], sums])
    third, pair = lax.optimization_barrier((far[2], pair))
    single = step(first_kernel, (rows, TILE), F32, "gram_third", [third])
    fourth, single = lax.optimization_barrier((far[3], single))
    own = step(last_kernel, (rows - 16 * tiles + 16, TILE), BF, "gram_last", [fourth, pair, single])
    other = lax.ppermute(own, "core", swap)
    own_share = lax.all_to_all(shares, ("z", "y", "x"), 0, 0, tiled=True)
    other_share = lax.ppermute(own_share, "core", swap)
    tail_in = (own, other, own_share, other_share, theta, incidence, inverse)
    activated, grad_features, grad_theta, grad_weight = pl.pallas_call(
        tail_kernel,
        out_shape=(
            jax.ShapeDtypeStruct((ent_dev, width), BF),
            jax.ShapeDtypeStruct((ent_dev, width), BF),
            jax.ShapeDtypeStruct((width, width), F32),
            jax.ShapeDtypeStruct((1, sec_dev), F32),
        ),
        in_specs=[vmem()] * len(tail_in),
        out_specs=(vmem(),) * 4,
        scratch_shapes=[
            pltpu.VMEM((ents, 2 * ents), BF),
            pltpu.VMEM((ents, 128), F32),
            pltpu.VMEM((2 * ents, width), BF),
            pltpu.VMEM((2 * ents, width), BF),
            pltpu.VMEM((ents, width), BF),
            pltpu.VMEM((ents, width), BF),
            pltpu.VMEM((layers * group, CORES, share, width), BF),
            pltpu.VMEM((layers * group, CORES, share, width), BF),
        ],
        compiler_params=params(),
        name="tail",
    )(*tail_in)
    return activated, grad_features, grad_theta, grad_weight.reshape(sec_dev)


def solution(mesh):
    ent, sec = mesh.shape["ent"], mesh.shape["sec"]
    dense = ent == 8 and sec == 4
    if dense:
        grid = Mesh(mesh.devices.reshape(ent // 2, 2, sec // CORES, CORES), ("z", "y", "x", "core"))
        whole, split = ("z", "y"), ("z", "y", "x", "core")
    else:
        grid = mesh
        whole, split = "ent", ("ent", "sec")
    placed = (
        P(whole, None),
        P(),
        P(split),
        P(split, None, None),
        P(split, None, None),
        P(split, None),
        P(whole, None),
    )
    return jax.shard_map(
        dense_body if dense else body,
        mesh=grid,
        in_specs=placed,
        out_specs=(P(whole, None), P(whole, None), P(), P(split)),
        check_vma=False,
    )
```

```python
import jax
import jax.numpy as jnp
from jax import lax
from jax.experimental import pallas as pl
from jax.experimental.pallas import tpu as pltpu
from jax.sharding import Mesh, PartitionSpec as P


def hot_table(indices, live_slots, offset, table_width):
    hits = (indices - offset)[:, None] == jnp.arange(table_width, dtype=jnp.int32)[None, :]
    return (hits & live_slots[:, None]).astype(jnp.bfloat16)


def body(features, theta, section_weight, pair_rows, pair_cols, pair_counts, cotangent):
    ent_dev = features.shape[0]
    feature_width = features.shape[1]
    sec_dev = section_weight.shape[0]
    blocks_count = pair_rows.shape[1]
    slot_count = pair_rows.shape[2]
    own_block = lax.axis_index("ent")
    row_lists = pair_rows[0]
    col_lists = pair_cols[0]
    usable = jnp.arange(slot_count, dtype=jnp.int32)[None, :] < pair_counts[0][:, None]
    usable_float = usable.astype(jnp.float32)
    entity_index = jnp.arange(blocks_count, dtype=jnp.int32)[:, None] * ent_dev + col_lists
    local_degree = jax.ops.segment_sum(
        usable_float.reshape(-1), entity_index.reshape(-1), num_segments=blocks_count * ent_dev
    )
    entity_degree = lax.psum(local_degree, ("ent", "sec"))
    own_degree = lax.dynamic_slice_in_dim(entity_degree, own_block * ent_dev, ent_dev)
    entity_scale = lax.rsqrt(1.0 + own_degree)[:, None]
    sec_count = jax.ops.segment_sum(
        usable_float.reshape(-1), row_lists.reshape(-1), num_segments=sec_dev
    )
    section_scale = (section_weight / (1.0 + sec_count))[:, None]

    def entity_fold(running, incoming, start_row):
        row_count = incoming.shape[0]
        span_width = min(row_count, ent_dev)
        block_span = max(row_count // ent_dev, 1)
        offset = start_row

        def add_block(turn_index, accum):
            row_slots = lax.dynamic_index_in_dim(row_lists, turn_index, 0, keepdims=False)
            col_slots = lax.dynamic_index_in_dim(col_lists, turn_index, 0, keepdims=False)
            live_slots = lax.dynamic_index_in_dim(usable, turn_index, 0, keepdims=False)
            values = lax.dynamic_slice_in_dim(incoming, turn_index * span_width, span_width, 0)
            col_hot = hot_table(col_slots, live_slots, offset, span_width)
            row_hot = hot_table(row_slots, live_slots, 0, sec_dev)
            picked = jnp.dot(col_hot, values, preferred_element_type=jnp.float32).astype(
                jnp.bfloat16
            )
            return accum + jnp.einsum(
                "ps,pf->sf", row_hot, picked, preferred_element_type=jnp.float32
            )

        return lax.fori_loop(0, block_span, add_block, running)

    def entity_terms(messages, start_row):
        span_width = min(lax.axis_size("ent") * ent_dev, ent_dev)
        block_span = max(lax.axis_size("ent") * ent_dev // ent_dev, 1)
        offset = start_row

        def block_term(turn_index):
            row_slots = lax.dynamic_index_in_dim(row_lists, turn_index, 0, keepdims=False)
            col_slots = lax.dynamic_index_in_dim(col_lists, turn_index, 0, keepdims=False)
            live_slots = lax.dynamic_index_in_dim(usable, turn_index, 0, keepdims=False)
            row_hot = hot_table(row_slots, live_slots, 0, sec_dev)
            col_hot = hot_table(col_slots, live_slots, offset, span_width)
            picked = jnp.dot(row_hot, messages, preferred_element_type=jnp.float32).astype(
                jnp.bfloat16
            )
            return jnp.einsum("pw,pf->wf", col_hot, picked, preferred_element_type=jnp.float32)

        pieces = lax.map(block_term, jnp.arange(block_span, dtype=jnp.int32))
        return pieces.reshape(block_span * span_width, feature_width)

    def collect(messages):
        partial_sum = lax.psum_scatter(
            entity_terms(messages, jnp.int32(0)), "ent", scatter_dimension=0, tiled=True
        )
        return lax.psum(partial_sum, "sec")

    zero_sections = jnp.zeros((sec_dev, feature_width), jnp.float32)
    projected = jnp.dot(features, theta, preferred_element_type=jnp.float32)
    scaled = (entity_scale * projected).astype(jnp.bfloat16)
    gathered = entity_fold(
        zero_sections, lax.all_gather(scaled, "ent", axis=0, tiled=True), jnp.int32(0)
    )
    messages = (section_scale * gathered).astype(jnp.bfloat16)
    collected = collect(messages)
    preact = entity_scale * collected
    activated = jax.nn.silu(preact).astype(jnp.bfloat16)
    sigmoid_pre = jax.nn.sigmoid(preact)
    grad_pre = cotangent.astype(jnp.float32) * sigmoid_pre * (1.0 + preact * (1.0 - sigmoid_pre))
    back_scaled = (entity_scale * grad_pre).astype(jnp.bfloat16)
    back_gathered = entity_fold(
        zero_sections, lax.all_gather(back_scaled, "ent", axis=0, tiled=True), jnp.int32(0)
    )
    grad_weight = jnp.sum(gathered * back_gathered, axis=1) / (1.0 + sec_count)
    back_messages = (section_scale * back_gathered).astype(jnp.bfloat16)
    back_collected = collect(back_messages)
    grad_proj = (entity_scale * back_collected).astype(jnp.bfloat16)
    grad_features = lax.dot_general(
        grad_proj, theta, (((1,), (1,)), ((), ())), preferred_element_type=jnp.float32
    ).astype(jnp.bfloat16)
    local_theta = lax.dot_general(
        features, grad_proj, (((0,), (0,)), ((), ())), preferred_element_type=jnp.float32
    )
    grad_theta = lax.psum(local_theta, "ent")
    return (activated, grad_features, grad_theta, grad_weight)


BF = jnp.bfloat16
F32 = jnp.float32
BIT = jnp.float8_e4m3fn
TILE = 256
SHIFT = TILE.bit_length() - 1
NT = (((1,), (1,)), ((), ()))
TN = (((0,), (0,)), ((), ()))
CORES = 2
CHUNKS = 4


def params(mebibytes=32):
    return pltpu.CompilerParams(vmem_limit_bytes=mebibytes * 2**20)


def vmem():
    return pl.BlockSpec(memory_space=pltpu.VMEM)


def hbm():
    return pl.BlockSpec(memory_space=pltpu.HBM)


def dot(a, b, dims=(((1,), (0,)), ((), ()))):
    return lax.dot_general(a, b, dims, preferred_element_type=F32)


def one_hot(index_row, count=TILE):
    ids = lax.broadcasted_iota(jnp.int32, (count, index_row.shape[1]), 0).astype(BF)
    return jnp.where(ids == index_row, jnp.ones((), BIT), jnp.zeros((), BIT))


def index_hot(lists, j, chunks):
    parts = [one_hot(lists[16 * c + j : 16 * c + j + 1, :]) for c in range(chunks)]
    return jnp.concatenate(parts, axis=1)


def column_to_row(column):
    wide = jnp.broadcast_to(column, (column.shape[0], 128))
    return wide.T[0:1, :]


def row_to_column(row):
    return jnp.broadcast_to(row, (128, 128)).T


def prep_kernel(
    counts, rows, cols, weight, features, cotangent, payload, inverse,
    counts_here, rows_here, cols_here, weight_here, share_here, sems,
):
    _, blocks, slots = rows.shape
    chunks = slots // 128
    ent_dev = features.shape[0]
    share = share_here.shape[0] // 2
    quarter = lax.axis_index("x") * CORES + lax.axis_index("core")
    here = pl.ds(pl.multiple_of(quarter * share, share), share)
    reads = [
        pltpu.make_async_copy(source, target, sems.at[n])
        for n, (source, target) in enumerate(
            (
                (counts, counts_here),
                (rows.at[0], rows_here),
                (cols.at[0], cols_here),
                (weight, weight_here),
                (features.at[here, :], share_here.at[0:share, :]),
                (cotangent.at[here, :], share_here.at[share : 2 * share, :]),
            )
        )
    ]
    for read in reads:
        read.start()
    for read in reads:
        read.wait()
    row_ids = rows_here[...]
    sub = lax.broadcasted_iota(jnp.int32, (blocks, slots), 0)
    lane = lax.broadcasted_iota(jnp.int32, (blocks, slots), 1)
    limit = jnp.zeros((blocks, slots), jnp.int32)
    for j in range(blocks):
        limit = jnp.where(sub == j, counts_here[0, j], limit)
    live = lane < limit
    part = lax.shift_right_logical(row_ids, SHIFT)
    high = jnp.where(live, part * ent_dev + cols_here[...], -1).astype(F32)
    low = jnp.where(live, row_ids & (TILE - 1), -1).astype(F32)
    part = part.astype(F32)
    degree = jnp.zeros((16, TILE), F32)
    for j in range(blocks):
        degree = degree + dot(
            one_hot(part[j : j + 1].astype(BF), 16), one_hot(low[j : j + 1].astype(BF)), NT
        )
    degree = jnp.concatenate([degree[0:1], degree[1:2]], axis=1)
    inverse[...] = 1.0 / (1.0 + degree)
    scale = weight_here[...] / (1.0 + degree)
    indices = jnp.concatenate([high, low], axis=0).astype(BF)
    for c in range(chunks):
        payload[16 * c : 16 * (c + 1), :] = indices[:, 128 * c : 128 * (c + 1)]
    ends = [scale[:, 128 * c : 128 * (c + 1)] for c in range(chunks)]
    ends.append(jnp.zeros((8 - chunks, 128), F32))
    at = 16 * chunks
    payload[at : at + 8, :] = jnp.concatenate(ends, axis=0).astype(BF)
    at += 8
    for n in range(2):
        for half in range(2):
            payload[at : at + share, :] = share_here[n * share : (n + 1) * share, half * 128 : (half + 1) * 128]
            at += share


def hold_kernel(source, target):
    target[...] = source[...]


def square(gram, full):
    ents = full.shape[0]
    start = 0
    for b in range(0, ents, TILE):
        for a in range(b, ents, TILE):
            piece = gram[start : start + TILE, :]
            full[a : a + TILE, b : b + TILE] = piece
            if a != b:
                full[b : b + TILE, a : a + TILE] = piece.T
            start += TILE


def own_kernel(payload, gram, incidence, full):
    ents = incidence.shape[1]
    ent_dev = TILE // (incidence.shape[0] // TILE)
    chunks = CHUNKS
    for j in range(ents // ent_dev):
        block = dot(index_hot(payload, 8 + j, chunks), index_hot(payload, j, chunks), NT).astype(BF)
        for half in range(2):
            incidence[half * TILE : (half + 1) * TILE, j * ent_dev : (j + 1) * ent_dev] = block[
                :, half * ent_dev : (half + 1) * ent_dev
            ]
    square(gram, full)


def collect_kernel(own, first, second, third, group):
    mine = lax.axis_index("z")
    for d, source in enumerate((own, first, second, third)):
        group[jnp.bitwise_xor(mine, d)] = source[...]


def column_rows(ents):
    spans, start = [], 0
    for b in range(ents // TILE):
        end = start + ents - b * TILE + 16
        spans.append((start, end))
        start = end
    return spans


def fill(lists, table, scaled):
    shards = lists.shape[0]
    chunks = CHUNKS
    ents = table.shape[0]
    sections = table.shape[1] // shards
    ent_dev = TILE // (sections // TILE)
    scaled[ents:, :] = jnp.ones((scaled.shape[0] - ents, scaled.shape[1]), BF)
    for q in range(shards):
        indices = lists.at[q]
        scale = jnp.concatenate(
            [indices[16 * chunks + c : 16 * chunks + c + 1, :] for c in range(chunks)], axis=1
        )
        for j in range(ents // ent_dev):
            block = dot(index_hot(indices, j, chunks), index_hot(indices, 8 + j, chunks), NT).astype(BF)
            rows = slice(j * ent_dev, (j + 1) * ent_dev)
            for half in range(2):
                at = q * sections + half * TILE
                part = block[half * ent_dev : (half + 1) * ent_dev, :]
                table[rows, at : at + TILE] = part
                scaled[rows, at : at + TILE] = part * scale[:, half * TILE : (half + 1) * TILE]


def column(b, table, scaled):
    return dot(scaled[b * TILE :, :], table[b * TILE : (b + 1) * TILE, :], NT)


def first_kernel(lists, sums, table, scaled):
    fill(lists, table, scaled)
    for b, (start, end) in enumerate(column_rows(table.shape[0])):
        sums[start:end, :] = column(b, table, scaled)


def second_kernel(lists, before, sums, table, scaled):
    fill(lists, table, scaled)
    for b, (start, end) in enumerate(column_rows(table.shape[0])):
        sums[start:end, :] = before[start:end, :] + column(b, table, scaled)


def last_kernel(lists, pair, single, near, third, gram, table, scaled):
    ents = table.shape[0]
    spans = column_rows(ents)
    fill(lists, table, scaled)
    at = 0
    degrees = []
    for b, (start, end) in enumerate(spans):
        size = end - start - 16
        total = pair[start:end, :] + (single[start:end, :] + column(b, table, scaled))
        gram[at : at + size, :] = total[0:size].astype(BF)
        at += size
        degree = total[size : size + 1]
        top = degree.astype(BF).astype(F32)
        degrees += [top, degree - top]
    degrees.append(jnp.zeros((16 - 2 * len(spans), TILE), F32))
    gram[at : at + 16, :] = jnp.concatenate(degrees, axis=0).astype(BF)
    at += 16
    for source in near + (third, lists):
        shards, height, _ = source.shape
        top = 16 * CHUNKS + 8
        share = (height - top) // 4
        for q in range(shards):
            for k in range(4):
                rows = slice(at + k // 2 * share, at + (k // 2 + 1) * share)
                gram[rows, k % 2 * 128 : k % 2 * 128 + 128] = source[q, top + k * share : top + (k + 1) * share, :]
            at += 2 * share


def tail_kernel(
    own, other, full, theta, incidence, inverse,
    activated, grad_features, grad_theta, grad_weight,
    rest, scale, values, backs, acts, feats, cots,
):
    ents = full.shape[0]
    tiles = ents // TILE
    ent_dev = activated.shape[0]
    width = theta.shape[0]
    share = feats.shape[2]
    per_group = feats.shape[0] // (ents // ent_dev)
    core = lax.axis_index("core")
    mine = lax.axis_index("z") * 2 + lax.axis_index("y")
    base = sum(ents - b * TILE for b in range(tiles))
    columns = lax.axis_size("y") * lax.axis_size("x")
    column_here = lax.axis_index("y") * 2 + lax.axis_index("x")
    for n, source in enumerate((own, other)):
        which = core if n == 0 else 1 - core
        at = base + 16
        for d in range(columns):
            there = jnp.bitwise_xor(column_here, d)
            for q in range(feats.shape[0] // columns):
                feats[q * columns + there, which] = source[at : at + share, :]
                cots[q * columns + there, which] = source[at + share : at + 2 * share, :]
                at += 2 * share
    degree_rows = own[base : base + 16, :].astype(F32) + other[base : base + 16, :].astype(F32)
    for b in range(tiles):
        row = lax.rsqrt(1.0 + (degree_rows[2 * b : 2 * b + 1] + degree_rows[2 * b + 1 : 2 * b + 2]))
        for h in range(TILE // 128):
            at = b * TILE + h * 128
            scale[at : at + 128, :] = row_to_column(row[:, h * 128 : (h + 1) * 128])
    square(other, rest)

    def es(at, rows):
        return jnp.concatenate([scale[at : at + rows, :]] * (width // 128), axis=1)

    def product(value, at, rows):
        return dot(full[at : at + rows, :], value[...]) + dot(rest[at : at + rows, :], value[...])

    every = feats[...].reshape(ents, width)
    for at in range(0, ents, TILE):
        span = slice(at, at + TILE)
        values[span, :] = (es(at, TILE) * dot(every[span, :], theta[...])).astype(BF)
    for at in range(0, ents, TILE):
        span = slice(at, at + TILE)
        preact = es(at, TILE) * product(values, at, TILE)
        gate = jax.nn.sigmoid(preact)
        acts[span, :] = (preact * gate).astype(BF)
        cot = cots[at // ent_dev * per_group : (at + TILE) // ent_dev * per_group].reshape(TILE, width).astype(F32)
        grad = cot * gate * (1.0 + preact * (1.0 - gate))
        backs[span, :] = (es(at, TILE) * grad).astype(BF)
    own_rows = pl.ds(pl.multiple_of(mine * ent_dev, ent_dev), ent_dev)
    activated[...] = acts[own_rows, :]
    for at in range(0, ents, TILE):
        acts[at : at + TILE, :] = (es(at, TILE) * product(backs, at, TILE)).astype(BF)
    grad_theta[...] = dot(every, acts[...], TN)
    grad_features[...] = dot(acts[own_rows, :], theta[...], NT).astype(BF)
    sections = incidence.shape[0]
    for q in range(0, sections, TILE):
        piece = incidence[q : q + TILE, :]
        both = dot(piece, values[...]) * dot(piece, backs[...])
        total = jnp.sum(both, axis=1, keepdims=True)
        grad_weight[:, q : q + TILE] = column_to_row(total) * inverse[:, q : q + TILE]


def dense_body(features, theta, section_weight, pair_rows, pair_cols, pair_counts, cotangent):
    ent_dev, width = features.shape
    sec_dev = section_weight.shape[0]
    _, blocks, slots = pair_rows.shape
    ents = blocks * ent_dev
    tiles = ents // TILE
    group = lax.axis_size("y") * lax.axis_size("x")
    layers = lax.axis_size("z")
    share = ent_dev // (lax.axis_size("x") * CORES)
    height = CHUNKS * 16 + 8
    swap = [(0, 1), (1, 0)]
    payload, inverse = pl.pallas_call(
        prep_kernel,
        out_shape=(
            jax.ShapeDtypeStruct((height + 4 * share, 128), BF),
            jax.ShapeDtypeStruct((1, sec_dev), F32),
        ),
        in_specs=[hbm()] * 6,
        out_specs=(vmem(), vmem()),
        scratch_shapes=[
            pltpu.SMEM((1, blocks), jnp.int32),
            pltpu.VMEM((blocks, slots), jnp.int32),
            pltpu.VMEM((blocks, slots), jnp.int32),
            pltpu.VMEM((1, sec_dev), F32),
            pltpu.VMEM((2 * share, width), BF),
            pltpu.SemaphoreType.DMA((6,)),
        ],
        compiler_params=params(63),
        name="prep",
    )(pair_counts, pair_rows, pair_cols, section_weight.reshape(1, sec_dev), features, cotangent)
    def layer(d):
        return lax.ppermute(payload, "z", [(i, i ^ d) for i in range(layers)])

    by_layer = [layer(d) for d in range(1, layers)]
    held = pl.pallas_call(
        hold_kernel,
        out_shape=jax.ShapeDtypeStruct(payload.shape, BF),
        in_specs=[vmem()],
        out_specs=vmem(),
        compiler_params=params(),
        name="hold",
    )(payload)
    near = pl.pallas_call(
        collect_kernel,
        out_shape=jax.ShapeDtypeStruct((group,) + payload.shape, BF),
        in_specs=[vmem()] * 4,
        out_specs=vmem(),
        compiler_params=params(),
        name="collect",
    )(held, *by_layer)

    far = [
        near,
        lax.ppermute(near, "x", swap),
        lax.ppermute(near, "y", swap),
        lax.ppermute(near, ("y", "x"), [(i, i ^ 3) for i in range(group)]),
    ]
    rows = column_rows(ents)[-1][1]
    scratch = [pltpu.VMEM((ents, group * sec_dev), BF), pltpu.VMEM((ents + 16, group * sec_dev), BF)]

    def step(kernel, shape, kind, name, inputs):
        return pl.pallas_call(
            kernel,
            out_shape=jax.ShapeDtypeStruct(shape, kind),
            in_specs=jax.tree.map(lambda _: vmem(), list(inputs)),
            out_specs=vmem(),
            scratch_shapes=scratch,
            compiler_params=params(),
            cost_estimate=pl.CostEstimate(
                flops=1000000000, bytes_accessed=1000, transcendentals=0
            ),
            name=name,
        )(*inputs)

    sums = step(first_kernel, (rows, TILE), F32, "gram_first", [far[0]])
    pair = step(second_kernel, (rows, TILE), F32, "gram_second", [far[1], sums])
    third, pair = lax.optimization_barrier((far[2], pair))
    single = step(first_kernel, (rows, TILE), F32, "gram_third", [third])
    fourth, single = lax.optimization_barrier((far[3], single))
    height = rows - 16 * tiles + 16 + layers * group * 2 * share
    own = step(last_kernel, (height, TILE), BF, "gram_last", [fourth, pair, single, tuple(far[:2]), third])
    other = lax.ppermute(own, "core", swap)
    incidence, full = pl.pallas_call(
        own_kernel,
        out_shape=(
            jax.ShapeDtypeStruct((sec_dev, ents), BF),
            jax.ShapeDtypeStruct((ents, ents), BF),
        ),
        in_specs=[vmem(), vmem()],
        out_specs=(vmem(), vmem()),
        compiler_params=params(),
        cost_estimate=pl.CostEstimate(flops=1000000000, bytes_accessed=1000, transcendentals=0),
        name="own_square",
    )(payload, own)
    tail_in = (own, other, full, theta, incidence, inverse)
    activated, grad_features, grad_theta, grad_weight = pl.pallas_call(
        tail_kernel,
        out_shape=(
            jax.ShapeDtypeStruct((ent_dev, width), BF),
            jax.ShapeDtypeStruct((ent_dev, width), BF),
            jax.ShapeDtypeStruct((width, width), F32),
            jax.ShapeDtypeStruct((1, sec_dev), F32),
        ),
        in_specs=[vmem()] * len(tail_in),
        out_specs=(vmem(),) * 4,
        scratch_shapes=[
            pltpu.VMEM((ents, ents), BF),
            pltpu.VMEM((ents, 128), F32),
            pltpu.VMEM((ents, width), BF),
            pltpu.VMEM((ents, width), BF),
            pltpu.VMEM((ents, width), BF),
            pltpu.VMEM((layers * group, CORES, share, width), BF),
            pltpu.VMEM((layers * group, CORES, share, width), BF),
        ],
        compiler_params=params(),
        name="tail",
    )(*tail_in)
    return activated, grad_features, grad_theta, grad_weight.reshape(sec_dev)


def solution(mesh):
    ent, sec = mesh.shape["ent"], mesh.shape["sec"]
    dense = ent == 8 and sec == 4
    if dense:
        grid = Mesh(mesh.devices.reshape(ent // 2, 2, sec // CORES, CORES), ("z", "y", "x", "core"))
        whole, split = ("z", "y"), ("z", "y", "x", "core")
    else:
        grid = mesh
        whole, split = "ent", ("ent", "sec")
    placed = (
        P(whole, None),
        P(),
        P(split),
        P(split, None, None),
        P(split, None, None),
        P(split, None),
        P(whole, None),
    )
    return jax.shard_map(
        dense_body if dense else body,
        mesh=grid,
        in_specs=placed,
        out_specs=(P(whole, None), P(whole, None), P(), P(split)),
        check_vma=False,
    )
```

```python
import jax
import jax.numpy as jnp
from jax import lax
from jax.experimental import pallas as pl
from jax.experimental.pallas import tpu as pltpu
from jax.sharding import Mesh, PartitionSpec as P


def hot_table(indices, live_slots, offset, table_width):
    hits = (indices - offset)[:, None] == jnp.arange(table_width, dtype=jnp.int32)[None, :]
    return (hits & live_slots[:, None]).astype(jnp.bfloat16)


def body(features, theta, section_weight, pair_rows, pair_cols, pair_counts, cotangent):
    ent_dev = features.shape[0]
    feature_width = features.shape[1]
    sec_dev = section_weight.shape[0]
    blocks_count = pair_rows.shape[1]
    slot_count = pair_rows.shape[2]
    own_block = lax.axis_index("ent")
    row_lists = pair_rows[0]
    col_lists = pair_cols[0]
    usable = jnp.arange(slot_count, dtype=jnp.int32)[None, :] < pair_counts[0][:, None]
    usable_float = usable.astype(jnp.float32)
    entity_index = jnp.arange(blocks_count, dtype=jnp.int32)[:, None] * ent_dev + col_lists
    local_degree = jax.ops.segment_sum(
        usable_float.reshape(-1), entity_index.reshape(-1), num_segments=blocks_count * ent_dev
    )
    entity_degree = lax.psum(local_degree, ("ent", "sec"))
    own_degree = lax.dynamic_slice_in_dim(entity_degree, own_block * ent_dev, ent_dev)
    entity_scale = lax.rsqrt(1.0 + own_degree)[:, None]
    sec_count = jax.ops.segment_sum(
        usable_float.reshape(-1), row_lists.reshape(-1), num_segments=sec_dev
    )
    section_scale = (section_weight / (1.0 + sec_count))[:, None]

    def entity_fold(running, incoming, start_row):
        row_count = incoming.shape[0]
        span_width = min(row_count, ent_dev)
        block_span = max(row_count // ent_dev, 1)
        offset = start_row

        def add_block(turn_index, accum):
            row_slots = lax.dynamic_index_in_dim(row_lists, turn_index, 0, keepdims=False)
            col_slots = lax.dynamic_index_in_dim(col_lists, turn_index, 0, keepdims=False)
            live_slots = lax.dynamic_index_in_dim(usable, turn_index, 0, keepdims=False)
            values = lax.dynamic_slice_in_dim(incoming, turn_index * span_width, span_width, 0)
            col_hot = hot_table(col_slots, live_slots, offset, span_width)
            row_hot = hot_table(row_slots, live_slots, 0, sec_dev)
            picked = jnp.dot(col_hot, values, preferred_element_type=jnp.float32).astype(
                jnp.bfloat16
            )
            return accum + jnp.einsum(
                "ps,pf->sf", row_hot, picked, preferred_element_type=jnp.float32
            )

        return lax.fori_loop(0, block_span, add_block, running)

    def entity_terms(messages, start_row):
        span_width = min(lax.axis_size("ent") * ent_dev, ent_dev)
        block_span = max(lax.axis_size("ent") * ent_dev // ent_dev, 1)
        offset = start_row

        def block_term(turn_index):
            row_slots = lax.dynamic_index_in_dim(row_lists, turn_index, 0, keepdims=False)
            col_slots = lax.dynamic_index_in_dim(col_lists, turn_index, 0, keepdims=False)
            live_slots = lax.dynamic_index_in_dim(usable, turn_index, 0, keepdims=False)
            row_hot = hot_table(row_slots, live_slots, 0, sec_dev)
            col_hot = hot_table(col_slots, live_slots, offset, span_width)
            picked = jnp.dot(row_hot, messages, preferred_element_type=jnp.float32).astype(
                jnp.bfloat16
            )
            return jnp.einsum("pw,pf->wf", col_hot, picked, preferred_element_type=jnp.float32)

        pieces = lax.map(block_term, jnp.arange(block_span, dtype=jnp.int32))
        return pieces.reshape(block_span * span_width, feature_width)

    def collect(messages):
        partial_sum = lax.psum_scatter(
            entity_terms(messages, jnp.int32(0)), "ent", scatter_dimension=0, tiled=True
        )
        return lax.psum(partial_sum, "sec")

    zero_sections = jnp.zeros((sec_dev, feature_width), jnp.float32)
    projected = jnp.dot(features, theta, preferred_element_type=jnp.float32)
    scaled = (entity_scale * projected).astype(jnp.bfloat16)
    gathered = entity_fold(
        zero_sections, lax.all_gather(scaled, "ent", axis=0, tiled=True), jnp.int32(0)
    )
    messages = (section_scale * gathered).astype(jnp.bfloat16)
    collected = collect(messages)
    preact = entity_scale * collected
    activated = jax.nn.silu(preact).astype(jnp.bfloat16)
    sigmoid_pre = jax.nn.sigmoid(preact)
    grad_pre = cotangent.astype(jnp.float32) * sigmoid_pre * (1.0 + preact * (1.0 - sigmoid_pre))
    back_scaled = (entity_scale * grad_pre).astype(jnp.bfloat16)
    back_gathered = entity_fold(
        zero_sections, lax.all_gather(back_scaled, "ent", axis=0, tiled=True), jnp.int32(0)
    )
    grad_weight = jnp.sum(gathered * back_gathered, axis=1) / (1.0 + sec_count)
    back_messages = (section_scale * back_gathered).astype(jnp.bfloat16)
    back_collected = collect(back_messages)
    grad_proj = (entity_scale * back_collected).astype(jnp.bfloat16)
    grad_features = lax.dot_general(
        grad_proj, theta, (((1,), (1,)), ((), ())), preferred_element_type=jnp.float32
    ).astype(jnp.bfloat16)
    local_theta = lax.dot_general(
        features, grad_proj, (((0,), (0,)), ((), ())), preferred_element_type=jnp.float32
    )
    grad_theta = lax.psum(local_theta, "ent")
    return (activated, grad_features, grad_theta, grad_weight)


BF = jnp.bfloat16
F32 = jnp.float32
BIT = jnp.float8_e4m3fn
TILE = 256
SHIFT = TILE.bit_length() - 1
NT = (((1,), (1,)), ((), ()))
TN = (((0,), (0,)), ((), ()))
CORES = 2
CHUNKS = 4


def params(mebibytes=32):
    return pltpu.CompilerParams(vmem_limit_bytes=mebibytes * 2**20)


def vmem():
    return pl.BlockSpec(memory_space=pltpu.VMEM)


def hbm():
    return pl.BlockSpec(memory_space=pltpu.HBM)


def dot(a, b, dims=(((1,), (0,)), ((), ()))):
    return lax.dot_general(a, b, dims, preferred_element_type=F32)


def one_hot(index_row, count=TILE):
    ids = lax.broadcasted_iota(jnp.int32, (count, index_row.shape[1]), 0).astype(BF)
    return jnp.where(ids == index_row, jnp.ones((), BIT), jnp.zeros((), BIT))


def index_hot(lists, j, chunks):
    parts = [one_hot(lists[16 * c + j : 16 * c + j + 1, :]) for c in range(chunks)]
    return jnp.concatenate(parts, axis=1)


def column_to_row(column):
    wide = jnp.broadcast_to(column, (column.shape[0], 128))
    return wide.T[0:1, :]


def row_to_column(row):
    return jnp.broadcast_to(row, (128, 128)).T


def prep_kernel(
    counts, rows, cols, weight, features, cotangent, payload, inverse,
    counts_here, rows_here, cols_here, weight_here, share_here, sems,
):
    _, blocks, slots = rows.shape
    chunks = slots // 128
    ent_dev = features.shape[0]
    share = share_here.shape[0] // 2
    quarter = lax.axis_index("x") * CORES + lax.axis_index("core")
    here = pl.ds(pl.multiple_of(quarter * share, share), share)
    reads = [
        pltpu.make_async_copy(source, target, sems.at[n])
        for n, (source, target) in enumerate(
            (
                (counts, counts_here),
                (rows.at[0], rows_here),
                (cols.at[0], cols_here),
                (weight, weight_here),
                (features.at[here, :], share_here.at[0:share, :]),
                (cotangent.at[here, :], share_here.at[share : 2 * share, :]),
            )
        )
    ]
    for read in reads:
        read.start()
    for read in reads:
        read.wait()
    row_ids = rows_here[...]
    sub = lax.broadcasted_iota(jnp.int32, (blocks, slots), 0)
    lane = lax.broadcasted_iota(jnp.int32, (blocks, slots), 1)
    limit = jnp.zeros((blocks, slots), jnp.int32)
    for j in range(blocks):
        limit = jnp.where(sub == j, counts_here[0, j], limit)
    live = lane < limit
    part = lax.shift_right_logical(row_ids, SHIFT)
    high = jnp.where(live, part * ent_dev + cols_here[...], -1).astype(F32)
    low = jnp.where(live, row_ids & (TILE - 1), -1).astype(F32)
    part = part.astype(F32)
    degree = jnp.zeros((16, TILE), F32)
    for j in range(blocks):
        degree = degree + dot(
            one_hot(part[j : j + 1].astype(BF), 16), one_hot(low[j : j + 1].astype(BF)), NT
        )
    degree = jnp.concatenate([degree[0:1], degree[1:2]], axis=1)
    inverse[...] = 1.0 / (1.0 + degree)
    scale = weight_here[...] / (1.0 + degree)
    indices = jnp.concatenate([high, low], axis=0).astype(BF)
    for c in range(chunks):
        payload[16 * c : 16 * (c + 1), :] = indices[:, 128 * c : 128 * (c + 1)]
    ends = [scale[:, 128 * c : 128 * (c + 1)] for c in range(chunks)]
    ends.append(jnp.zeros((8 - chunks, 128), F32))
    at = 16 * chunks
    payload[at : at + 8, :] = jnp.concatenate(ends, axis=0).astype(BF)
    at += 8
    for n in range(2):
        for half in range(2):
            payload[at : at + share, :] = share_here[n * share : (n + 1) * share, half * 128 : (half + 1) * 128]
            at += share


def hold_kernel(source, target):
    target[...] = source[...]


def square(firsts, others, full):
    ents = full.shape[0]
    start = 0
    for b in range(0, ents, TILE):
        for a in range(b, ents, TILE):
            refs, at = (firsts, a) if b == 0 else (others, start)
            parts = [ref[at : at + TILE, :].astype(F32) for ref in refs]
            piece = (parts[0] + parts[1]).astype(BF)
            full[a : a + TILE, b : b + TILE] = piece
            if a != b:
                full[b : b + TILE, a : a + TILE] = piece.T
            start += TILE if b else 0


def middle_kernel(payload, own_first, other_first, theta, incidence, feats, cots, projected):
    ents = incidence.shape[1]
    ent_dev = TILE // (incidence.shape[0] // TILE)
    chunks = CHUNKS
    share = feats.shape[2]
    core = lax.axis_index("core")
    columns = lax.axis_size("y") * lax.axis_size("x")
    column_here = lax.axis_index("y") * 2 + lax.axis_index("x")
    for n, source in enumerate((own_first, other_first)):
        which = core if n == 0 else 1 - core
        at = ents
        for d in range(columns):
            there = jnp.bitwise_xor(column_here, d)
            for q in range(feats.shape[0] // columns):
                feats[q * columns + there, which] = source[at : at + share, :]
                cots[q * columns + there, which] = source[at + share : at + 2 * share, :]
                at += 2 * share
    for j in range(ents // ent_dev):
        block = dot(index_hot(payload, 8 + j, chunks), index_hot(payload, j, chunks), NT).astype(BF)
        for half in range(2):
            incidence[half * TILE : (half + 1) * TILE, j * ent_dev : (j + 1) * ent_dev] = block[
                :, half * ent_dev : (half + 1) * ent_dev
            ]
    every = feats[...].reshape(ents, theta.shape[0])
    projected[...] = dot(every, theta[...])


def collect_kernel(own, first, second, third, group):
    mine = lax.axis_index("z")
    for d, source in enumerate((own, first, second, third)):
        group[jnp.bitwise_xor(mine, d)] = source[...]


def column_rows(ents):
    spans, start = [], 0
    for b in range(ents // TILE):
        end = start + ents - b * TILE + 16
        spans.append((start, end))
        start = end
    return spans


def fill(lists, table, scaled):
    shards = lists.shape[0]
    chunks = CHUNKS
    ents = table.shape[0]
    sections = table.shape[1] // shards
    ent_dev = TILE // (sections // TILE)
    scaled[ents:, :] = jnp.ones((scaled.shape[0] - ents, scaled.shape[1]), BF)
    for q in range(shards):
        indices = lists.at[q]
        scale = jnp.concatenate(
            [indices[16 * chunks + c : 16 * chunks + c + 1, :] for c in range(chunks)], axis=1
        )
        for j in range(ents // ent_dev):
            block = dot(index_hot(indices, j, chunks), index_hot(indices, 8 + j, chunks), NT).astype(BF)
            rows = slice(j * ent_dev, (j + 1) * ent_dev)
            for half in range(2):
                at = q * sections + half * TILE
                part = block[half * ent_dev : (half + 1) * ent_dev, :]
                table[rows, at : at + TILE] = part
                scaled[rows, at : at + TILE] = part * scale[:, half * TILE : (half + 1) * TILE]


def column(b, table, scaled):
    return dot(scaled[b * TILE :, :], table[b * TILE : (b + 1) * TILE, :], NT)


def first_kernel(lists, sums, table, scaled):
    fill(lists, table, scaled)
    for b, (start, end) in enumerate(column_rows(table.shape[0])):
        sums[start:end, :] = column(b, table, scaled)


def second_kernel(lists, before, sums, table, scaled):
    fill(lists, table, scaled)
    for b, (start, end) in enumerate(column_rows(table.shape[0])):
        sums[start:end, :] = before[start:end, :] + column(b, table, scaled)


def last_kernel(lists, pair, single, near, third, first, table, scaled):
    ents = table.shape[0]
    fill(lists, table, scaled)
    total = pair[0:ents, :] + (single[0:ents, :] + dot(scaled[0:ents, :], table[0:TILE, :], NT))
    first[0:ents, :] = total.astype(BF)
    at = ents
    for source in near + (third, lists):
        shards, height, _ = source.shape
        top = 16 * CHUNKS + 8
        share = (height - top) // 4
        for q in range(shards):
            for k in range(4):
                rows = slice(at + k // 2 * share, at + (k // 2 + 1) * share)
                first[rows, k % 2 * 128 : k % 2 * 128 + 128] = source[q, top + k * share : top + (k + 1) * share, :]
            at += 2 * share


def others_kernel(table, scaled, pair, single, others):
    ents = table.shape[0]
    at = 0
    degrees = []
    for b, (start, end) in enumerate(column_rows(ents)):
        size = end - start - 16
        if b == 0:
            start, size = end - 16, 0
            product = dot(scaled[ents:, :], table[0:TILE, :], NT)
        else:
            product = column(b, table, scaled)
        total = pair[start:end, :] + (single[start:end, :] + product)
        if b:
            others[at : at + size, :] = total[0:size].astype(BF)
        at += size
        degree = total[size : size + 1]
        top = degree.astype(BF).astype(F32)
        degrees += [top, degree - top]
    degrees.append(jnp.zeros((16 - len(degrees), TILE), F32))
    others[at : at + 16, :] = jnp.concatenate(degrees, axis=0).astype(BF)


def tail_kernel(
    own_first, own_others, other_first, other_others, feats, cots, projected, theta, incidence, inverse,
    activated, grad_features, grad_theta, grad_weight,
    full, scale, values, backs, acts,
):
    ents = full.shape[0]
    tiles = ents // TILE
    ent_dev = activated.shape[0]
    width = theta.shape[0]
    per_group = feats.shape[0] // (ents // ent_dev)
    mine = lax.axis_index("z") * 2 + lax.axis_index("y")
    base = own_others.shape[0] - 16
    degree_rows = own_others[base:, :].astype(F32) + other_others[base:, :].astype(F32)
    for b in range(tiles):
        row = lax.rsqrt(1.0 + (degree_rows[2 * b : 2 * b + 1] + degree_rows[2 * b + 1 : 2 * b + 2]))
        for h in range(TILE // 128):
            at = b * TILE + h * 128
            scale[at : at + 128, :] = row_to_column(row[:, h * 128 : (h + 1) * 128])
    square((own_first, other_first), (own_others, other_others), full)

    def es(at, rows):
        return jnp.concatenate([scale[at : at + rows, :]] * (width // 128), axis=1)

    def product(value, at, rows):
        return dot(full[at : at + rows, :], value[...])

    for at in range(0, ents, TILE):
        span = slice(at, at + TILE)
        values[span, :] = (es(at, TILE) * projected[span, :]).astype(BF)
    for at in range(0, ents, TILE):
        span = slice(at, at + TILE)
        preact = es(at, TILE) * product(values, at, TILE)
        gate = jax.nn.sigmoid(preact)
        acts[span, :] = (preact * gate).astype(BF)
        cot = cots[at // ent_dev * per_group : (at + TILE) // ent_dev * per_group].reshape(TILE, width).astype(F32)
        grad = cot * gate * (1.0 + preact * (1.0 - gate))
        backs[span, :] = (es(at, TILE) * grad).astype(BF)
    own_rows = pl.ds(pl.multiple_of(mine * ent_dev, ent_dev), ent_dev)
    activated[...] = acts[own_rows, :]
    for at in range(0, ents, TILE):
        acts[at : at + TILE, :] = (es(at, TILE) * product(backs, at, TILE)).astype(BF)
    grad_theta[...] = dot(feats[...].reshape(ents, width), acts[...], TN)
    grad_features[...] = dot(acts[own_rows, :], theta[...], NT).astype(BF)
    sections = incidence.shape[0]
    for q in range(0, sections, TILE):
        piece = incidence[q : q + TILE, :]
        both = dot(piece, values[...]) * dot(piece, backs[...])
        total = jnp.sum(both, axis=1, keepdims=True)
        grad_weight[:, q : q + TILE] = column_to_row(total) * inverse[:, q : q + TILE]


def dense_body(features, theta, section_weight, pair_rows, pair_cols, pair_counts, cotangent):
    ent_dev, width = features.shape
    sec_dev = section_weight.shape[0]
    _, blocks, slots = pair_rows.shape
    ents = blocks * ent_dev
    tiles = ents // TILE
    group = lax.axis_size("y") * lax.axis_size("x")
    layers = lax.axis_size("z")
    share = ent_dev // (lax.axis_size("x") * CORES)
    height = CHUNKS * 16 + 8
    swap = [(0, 1), (1, 0)]
    payload, inverse = pl.pallas_call(
        prep_kernel,
        out_shape=(
            jax.ShapeDtypeStruct((height + 4 * share, 128), BF),
            jax.ShapeDtypeStruct((1, sec_dev), F32),
        ),
        in_specs=[hbm()] * 6,
        out_specs=(vmem(), vmem()),
        scratch_shapes=[
            pltpu.SMEM((1, blocks), jnp.int32),
            pltpu.VMEM((blocks, slots), jnp.int32),
            pltpu.VMEM((blocks, slots), jnp.int32),
            pltpu.VMEM((1, sec_dev), F32),
            pltpu.VMEM((2 * share, width), BF),
            pltpu.SemaphoreType.DMA((6,)),
        ],
        compiler_params=params(63),
        name="prep",
    )(pair_counts, pair_rows, pair_cols, section_weight.reshape(1, sec_dev), features, cotangent)
    def layer(d):
        return lax.ppermute(payload, "z", [(i, i ^ d) for i in range(layers)])

    by_layer = [layer(d) for d in range(1, layers)]
    held = pl.pallas_call(
        hold_kernel,
        out_shape=jax.ShapeDtypeStruct(payload.shape, BF),
        in_specs=[vmem()],
        out_specs=vmem(),
        compiler_params=params(),
        name="hold",
    )(payload)
    near = pl.pallas_call(
        collect_kernel,
        out_shape=jax.ShapeDtypeStruct((group,) + payload.shape, BF),
        in_specs=[vmem()] * 4,
        out_specs=vmem(),
        compiler_params=params(),
        name="collect",
    )(held, *by_layer)

    far = [
        near,
        lax.ppermute(near, "x", swap),
        lax.ppermute(near, "y", swap),
        lax.ppermute(near, ("y", "x"), [(i, i ^ 3) for i in range(group)]),
    ]
    rows = column_rows(ents)[-1][1]
    scratch = [pltpu.VMEM((ents, group * sec_dev), BF), pltpu.VMEM((ents + 16, group * sec_dev), BF)]

    def step(kernel, shape, kind, name, inputs):
        return pl.pallas_call(
            kernel,
            out_shape=jax.ShapeDtypeStruct(shape, kind),
            in_specs=jax.tree.map(lambda _: vmem(), list(inputs)),
            out_specs=vmem(),
            scratch_shapes=scratch,
            compiler_params=params(),
            cost_estimate=pl.CostEstimate(
                flops=1000000000, bytes_accessed=1000, transcendentals=0
            ),
            name=name,
        )(*inputs)

    sums = step(first_kernel, (rows, TILE), F32, "gram_first", [far[0]])
    pair = step(second_kernel, (rows, TILE), F32, "gram_second", [far[1], sums])
    third, pair = lax.optimization_barrier((far[2], pair))
    single = step(first_kernel, (rows, TILE), F32, "gram_third", [third])
    fourth, single = lax.optimization_barrier((far[3], single))
    def plain(kernel, outs, name, inputs):
        return pl.pallas_call(
            kernel,
            out_shape=[jax.ShapeDtypeStruct(shape, kind) for shape, kind in outs],
            in_specs=jax.tree.map(lambda _: vmem(), list(inputs)),
            out_specs=[vmem()] * len(outs),
            compiler_params=params(),
            cost_estimate=pl.CostEstimate(flops=1000000000, bytes_accessed=1000, transcendentals=0),
            name=name,
        )(*inputs)

    own_first, table, scaled = plain(
        last_kernel,
        [
            ((ents + layers * group * 2 * share, TILE), BF),
            ((ents, group * sec_dev), BF),
            ((ents + 16, group * sec_dev), BF),
        ],
        "gram_last",
        [fourth, pair, single, tuple(far[:2]), third],
    )
    other_first = lax.ppermute(own_first, "core", swap)
    (own_others,) = plain(
        others_kernel, [((rows - 16 * tiles - ents + 16, TILE), BF)], "gram_others", [table, scaled, pair, single]
    )
    other_others = lax.ppermute(own_others, "core", swap)
    stack = (layers * group, CORES, share, width)
    incidence, feats, cots, projected = plain(
        middle_kernel,
        [((sec_dev, ents), BF), (stack, BF), (stack, BF), ((ents, width), F32)],
        "middle",
        [payload, own_first, other_first, theta],
    )
    tail_in = (own_first, own_others, other_first, other_others, feats, cots, projected, theta, incidence, inverse)
    activated, grad_features, grad_theta, grad_weight = pl.pallas_call(
        tail_kernel,
        out_shape=(
            jax.ShapeDtypeStruct((ent_dev, width), BF),
            jax.ShapeDtypeStruct((ent_dev, width), BF),
            jax.ShapeDtypeStruct((width, width), F32),
            jax.ShapeDtypeStruct((1, sec_dev), F32),
        ),
        in_specs=[vmem()] * len(tail_in),
        out_specs=(vmem(),) * 4,
        scratch_shapes=[
            pltpu.VMEM((ents, ents), BF),
            pltpu.VMEM((ents, 128), F32),
            pltpu.VMEM((ents, width), BF),
            pltpu.VMEM((ents, width), BF),
            pltpu.VMEM((ents, width), BF),
        ],
        compiler_params=params(),
        name="tail",
    )(*tail_in)
    return activated, grad_features, grad_theta, grad_weight.reshape(sec_dev)


def solution(mesh):
    ent, sec = mesh.shape["ent"], mesh.shape["sec"]
    dense = ent == 8 and sec == 4
    if dense:
        grid = Mesh(mesh.devices.reshape(ent // 2, 2, sec // CORES, CORES), ("z", "y", "x", "core"))
        whole, split = ("z", "y"), ("z", "y", "x", "core")
    else:
        grid = mesh
        whole, split = "ent", ("ent", "sec")
    placed = (
        P(whole, None),
        P(),
        P(split),
        P(split, None, None),
        P(split, None, None),
        P(split, None),
        P(whole, None),
    )
    return jax.shard_map(
        dense_body if dense else body,
        mesh=grid,
        in_specs=placed,
        out_specs=(P(whole, None), P(whole, None), P(), P(split)),
        check_vma=False,
    )
```

```python
import jax
import jax.numpy as jnp
from jax import lax
from jax.experimental import pallas as pl
from jax.experimental.pallas import tpu as pltpu
from jax.sharding import Mesh, PartitionSpec as P


def hot_table(indices, live_slots, offset, table_width):
    hits = (indices - offset)[:, None] == jnp.arange(table_width, dtype=jnp.int32)[None, :]
    return (hits & live_slots[:, None]).astype(jnp.bfloat16)


def body(features, theta, section_weight, pair_rows, pair_cols, pair_counts, cotangent):
    ent_dev = features.shape[0]
    feature_width = features.shape[1]
    sec_dev = section_weight.shape[0]
    blocks_count = pair_rows.shape[1]
    slot_count = pair_rows.shape[2]
    own_block = lax.axis_index("ent")
    row_lists = pair_rows[0]
    col_lists = pair_cols[0]
    usable = jnp.arange(slot_count, dtype=jnp.int32)[None, :] < pair_counts[0][:, None]
    usable_float = usable.astype(jnp.float32)
    entity_index = jnp.arange(blocks_count, dtype=jnp.int32)[:, None] * ent_dev + col_lists
    local_degree = jax.ops.segment_sum(
        usable_float.reshape(-1), entity_index.reshape(-1), num_segments=blocks_count * ent_dev
    )
    entity_degree = lax.psum(local_degree, ("ent", "sec"))
    own_degree = lax.dynamic_slice_in_dim(entity_degree, own_block * ent_dev, ent_dev)
    entity_scale = lax.rsqrt(1.0 + own_degree)[:, None]
    sec_count = jax.ops.segment_sum(
        usable_float.reshape(-1), row_lists.reshape(-1), num_segments=sec_dev
    )
    section_scale = (section_weight / (1.0 + sec_count))[:, None]

    def entity_fold(running, incoming, start_row):
        row_count = incoming.shape[0]
        span_width = min(row_count, ent_dev)
        block_span = max(row_count // ent_dev, 1)
        offset = start_row

        def add_block(turn_index, accum):
            row_slots = lax.dynamic_index_in_dim(row_lists, turn_index, 0, keepdims=False)
            col_slots = lax.dynamic_index_in_dim(col_lists, turn_index, 0, keepdims=False)
            live_slots = lax.dynamic_index_in_dim(usable, turn_index, 0, keepdims=False)
            values = lax.dynamic_slice_in_dim(incoming, turn_index * span_width, span_width, 0)
            col_hot = hot_table(col_slots, live_slots, offset, span_width)
            row_hot = hot_table(row_slots, live_slots, 0, sec_dev)
            picked = jnp.dot(col_hot, values, preferred_element_type=jnp.float32).astype(
                jnp.bfloat16
            )
            return accum + jnp.einsum(
                "ps,pf->sf", row_hot, picked, preferred_element_type=jnp.float32
            )

        return lax.fori_loop(0, block_span, add_block, running)

    def entity_terms(messages, start_row):
        span_width = min(lax.axis_size("ent") * ent_dev, ent_dev)
        block_span = max(lax.axis_size("ent") * ent_dev // ent_dev, 1)
        offset = start_row

        def block_term(turn_index):
            row_slots = lax.dynamic_index_in_dim(row_lists, turn_index, 0, keepdims=False)
            col_slots = lax.dynamic_index_in_dim(col_lists, turn_index, 0, keepdims=False)
            live_slots = lax.dynamic_index_in_dim(usable, turn_index, 0, keepdims=False)
            row_hot = hot_table(row_slots, live_slots, 0, sec_dev)
            col_hot = hot_table(col_slots, live_slots, offset, span_width)
            picked = jnp.dot(row_hot, messages, preferred_element_type=jnp.float32).astype(
                jnp.bfloat16
            )
            return jnp.einsum("pw,pf->wf", col_hot, picked, preferred_element_type=jnp.float32)

        pieces = lax.map(block_term, jnp.arange(block_span, dtype=jnp.int32))
        return pieces.reshape(block_span * span_width, feature_width)

    def collect(messages):
        partial_sum = lax.psum_scatter(
            entity_terms(messages, jnp.int32(0)), "ent", scatter_dimension=0, tiled=True
        )
        return lax.psum(partial_sum, "sec")

    zero_sections = jnp.zeros((sec_dev, feature_width), jnp.float32)
    projected = jnp.dot(features, theta, preferred_element_type=jnp.float32)
    scaled = (entity_scale * projected).astype(jnp.bfloat16)
    gathered = entity_fold(
        zero_sections, lax.all_gather(scaled, "ent", axis=0, tiled=True), jnp.int32(0)
    )
    messages = (section_scale * gathered).astype(jnp.bfloat16)
    collected = collect(messages)
    preact = entity_scale * collected
    activated = jax.nn.silu(preact).astype(jnp.bfloat16)
    sigmoid_pre = jax.nn.sigmoid(preact)
    grad_pre = cotangent.astype(jnp.float32) * sigmoid_pre * (1.0 + preact * (1.0 - sigmoid_pre))
    back_scaled = (entity_scale * grad_pre).astype(jnp.bfloat16)
    back_gathered = entity_fold(
        zero_sections, lax.all_gather(back_scaled, "ent", axis=0, tiled=True), jnp.int32(0)
    )
    grad_weight = jnp.sum(gathered * back_gathered, axis=1) / (1.0 + sec_count)
    back_messages = (section_scale * back_gathered).astype(jnp.bfloat16)
    back_collected = collect(back_messages)
    grad_proj = (entity_scale * back_collected).astype(jnp.bfloat16)
    grad_features = lax.dot_general(
        grad_proj, theta, (((1,), (1,)), ((), ())), preferred_element_type=jnp.float32
    ).astype(jnp.bfloat16)
    local_theta = lax.dot_general(
        features, grad_proj, (((0,), (0,)), ((), ())), preferred_element_type=jnp.float32
    )
    grad_theta = lax.psum(local_theta, "ent")
    return (activated, grad_features, grad_theta, grad_weight)


BF = jnp.bfloat16
F32 = jnp.float32
BIT = jnp.float8_e4m3fn
TILE = 256
SHIFT = TILE.bit_length() - 1
NT = (((1,), (1,)), ((), ()))
TN = (((0,), (0,)), ((), ()))
CORES = 2
CHUNKS = 4


def params(mebibytes=32):
    return pltpu.CompilerParams(vmem_limit_bytes=mebibytes * 2**20)


def vmem():
    return pl.BlockSpec(memory_space=pltpu.VMEM)


def hbm():
    return pl.BlockSpec(memory_space=pltpu.HBM)


def dot(a, b, dims=(((1,), (0,)), ((), ()))):
    return lax.dot_general(a, b, dims, preferred_element_type=F32)


def one_hot(index_row, count=TILE):
    ids = lax.broadcasted_iota(jnp.int32, (count, index_row.shape[1]), 0).astype(BF)
    return jnp.where(ids == index_row, jnp.ones((), BIT), jnp.zeros((), BIT))


def index_hot(lists, j, chunks):
    parts = [one_hot(lists[16 * c + j : 16 * c + j + 1, :]) for c in range(chunks)]
    return jnp.concatenate(parts, axis=1)


def column_to_row(column):
    wide = jnp.broadcast_to(column, (column.shape[0], 128))
    return wide.T[0:1, :]


def row_to_column(row):
    return jnp.broadcast_to(row, (128, 128)).T


def prep_kernel(
    counts, rows, cols, weight, features, cotangent, payload, inverse,
    counts_here, rows_here, cols_here, weight_here, share_here, sems,
):
    _, blocks, slots = rows.shape
    chunks = slots // 128
    ent_dev = features.shape[0]
    share = share_here.shape[0] // 2
    quarter = lax.axis_index("x") * CORES + lax.axis_index("core")
    here = pl.ds(pl.multiple_of(quarter * share, share), share)
    reads = [
        pltpu.make_async_copy(source, target, sems.at[n])
        for n, (source, target) in enumerate(
            (
                (counts, counts_here),
                (rows.at[0], rows_here),
                (cols.at[0], cols_here),
                (weight, weight_here),
                (features.at[here, :], share_here.at[0:share, :]),
                (cotangent.at[here, :], share_here.at[share : 2 * share, :]),
            )
        )
    ]
    for read in reads:
        read.start()
    for read in reads:
        read.wait()
    row_ids = rows_here[...]
    sub = lax.broadcasted_iota(jnp.int32, (blocks, slots), 0)
    lane = lax.broadcasted_iota(jnp.int32, (blocks, slots), 1)
    limit = jnp.zeros((blocks, slots), jnp.int32)
    for j in range(blocks):
        limit = jnp.where(sub == j, counts_here[0, j], limit)
    live = lane < limit
    part = lax.shift_right_logical(row_ids, SHIFT)
    high = jnp.where(live, part * ent_dev + cols_here[...], -1).astype(F32)
    low = jnp.where(live, row_ids & (TILE - 1), -1).astype(F32)
    part = part.astype(F32)
    degree = jnp.zeros((16, TILE), F32)
    for j in range(blocks):
        degree = degree + dot(
            one_hot(part[j : j + 1].astype(BF), 16), one_hot(low[j : j + 1].astype(BF)), NT
        )
    degree = jnp.concatenate([degree[0:1], degree[1:2]], axis=1)
    inverse[...] = 1.0 / (1.0 + degree)
    scale = weight_here[...] / (1.0 + degree)
    indices = jnp.concatenate([high, low], axis=0).astype(BF)
    for c in range(chunks):
        payload[16 * c : 16 * (c + 1), :] = indices[:, 128 * c : 128 * (c + 1)]
    ends = [scale[:, 128 * c : 128 * (c + 1)] for c in range(chunks)]
    ends.append(jnp.zeros((8 - chunks, 128), F32))
    at = 16 * chunks
    payload[at : at + 8, :] = jnp.concatenate(ends, axis=0).astype(BF)
    at += 8
    for n in range(2):
        for half in range(2):
            payload[at : at + share, :] = share_here[n * share : (n + 1) * share, half * 128 : (half + 1) * 128]
            at += share


def hold_kernel(source, target):
    target[...] = source[...]


def square(firsts, others, full):
    ents = full.shape[0]
    start = 0
    for b in range(0, ents, TILE):
        for a in range(b, ents, TILE):
            refs, at = (firsts, a) if b == 0 else (others, start)
            parts = [ref[at : at + TILE, :].astype(F32) for ref in refs]
            piece = (parts[0] + parts[1]).astype(BF)
            full[a : a + TILE, b : b + TILE] = piece
            if a != b:
                full[b : b + TILE, a : a + TILE] = piece.T
            start += TILE if b else 0


def middle_kernel(payload, own_first, other_first, theta, incidence, feats, cots, projected):
    ents = incidence.shape[1]
    ent_dev = TILE // (incidence.shape[0] // TILE)
    chunks = CHUNKS
    share = feats.shape[2]
    core = lax.axis_index("core")
    columns = lax.axis_size("y") * lax.axis_size("x")
    column_here = lax.axis_index("y") * 2 + lax.axis_index("x")
    for n, source in enumerate((own_first, other_first)):
        which = core if n == 0 else 1 - core
        at = ents
        for d in range(columns):
            there = jnp.bitwise_xor(column_here, d)
            for q in range(feats.shape[0] // columns):
                feats[q * columns + there, which] = source[at : at + share, :]
                cots[q * columns + there, which] = source[at + share : at + 2 * share, :]
                at += 2 * share
    for j in range(ents // ent_dev):
        block = dot(index_hot(payload, 8 + j, chunks), index_hot(payload, j, chunks), NT).astype(BF)
        for half in range(2):
            incidence[half * TILE : (half + 1) * TILE, j * ent_dev : (j + 1) * ent_dev] = block[
                :, half * ent_dev : (half + 1) * ent_dev
            ]
    every = feats[...].reshape(ents, theta.shape[0])
    projected[...] = dot(every, theta[...])


def collect_kernel(own, first, second, third, group):
    mine = lax.axis_index("z")
    for d, source in enumerate((own, first, second, third)):
        group[jnp.bitwise_xor(mine, d)] = source[...]


def column_rows(ents):
    spans, start = [], 0
    for b in range(ents // TILE):
        end = start + ents - b * TILE + 16
        spans.append((start, end))
        start = end
    return spans


def members(group):
    return [group.at[q] for q in range(group.shape[0])]


def fill(shards, table, scaled):
    chunks = CHUNKS
    ents = table.shape[0]
    sections = table.shape[1] // len(shards)
    ent_dev = TILE // (sections // TILE)
    scaled[ents:, :] = jnp.ones((scaled.shape[0] - ents, scaled.shape[1]), BF)
    for q, indices in enumerate(shards):
        scale = jnp.concatenate(
            [indices[16 * chunks + c : 16 * chunks + c + 1, :] for c in range(chunks)], axis=1
        )
        for j in range(ents // ent_dev):
            block = dot(index_hot(indices, j, chunks), index_hot(indices, 8 + j, chunks), NT).astype(BF)
            rows = slice(j * ent_dev, (j + 1) * ent_dev)
            for half in range(2):
                at = q * sections + half * TILE
                part = block[half * ent_dev : (half + 1) * ent_dev, :]
                table[rows, at : at + TILE] = part
                scaled[rows, at : at + TILE] = part * scale[:, half * TILE : (half + 1) * TILE]


def column(b, table, scaled):
    return dot(scaled[b * TILE :, :], table[b * TILE : (b + 1) * TILE, :], NT)


def shards_kernel(shards, sums, table, scaled):
    fill(shards, table, scaled)
    for b, (start, end) in enumerate(column_rows(table.shape[0])):
        sums[start:end, :] = column(b, table, scaled)


def own_kernel(payload, sums, table, scaled):
    shards_kernel([payload], sums, table, scaled)


def third_kernel(group, sums, table, scaled):
    shards_kernel(members(group), sums, table, scaled)


def layers_kernel(arrived, before, sums, table, scaled):
    fill(arrived, table, scaled)
    for b, (start, end) in enumerate(column_rows(table.shape[0])):
        sums[start:end, :] = before[start:end, :] + column(b, table, scaled)


def second_kernel(group, before, sums, table, scaled):
    layers_kernel(members(group), before, sums, table, scaled)


def degree_rows(*rows):
    out = []
    for row in rows:
        top = row.astype(BF).astype(F32)
        out += [top, row - top]
    out.append(jnp.zeros((16 - len(out), TILE), F32))
    return jnp.concatenate(out, axis=0).astype(BF)


def last_kernel(lists, pair, single, near, third, first, table, scaled):
    ents = table.shape[0]
    fill(members(lists), table, scaled)
    start, end = column_rows(ents)[0]
    total = pair[start:end, :] + (single[start:end, :] + column(0, table, scaled))
    first[0:ents, :] = total[0:ents].astype(BF)
    first[first.shape[0] - 16 :, :] = degree_rows(total[ents : ents + 1])
    at = ents
    for source in near + (third, lists):
        shards, height, _ = source.shape
        top = 16 * CHUNKS + 8
        share = (height - top) // 4
        for q in range(shards):
            for k in range(4):
                rows = slice(at + k // 2 * share, at + (k // 2 + 1) * share)
                first[rows, k % 2 * 128 : k % 2 * 128 + 128] = source[q, top + k * share : top + (k + 1) * share, :]
            at += 2 * share


def others_kernel(table, scaled, pair, single, others):
    ents = table.shape[0]
    at = 0
    degrees = []
    for b, (start, end) in enumerate(column_rows(ents)):
        if b:
            size = end - start - 16
            total = pair[start:end, :] + (single[start:end, :] + column(b, table, scaled))
            others[at : at + size, :] = total[0:size].astype(BF)
            at += size
            degrees.append(total[size : size + 1])
    others[at : at + 16, :] = degree_rows(*degrees)


def tail_kernel(
    own_first, own_others, other_first, other_others, feats, cots, projected, theta, incidence, inverse,
    activated, grad_features, grad_theta, grad_weight,
    full, scale, values, backs, acts,
):
    ents = full.shape[0]
    tiles = ents // TILE
    ent_dev = activated.shape[0]
    width = theta.shape[0]
    per_group = feats.shape[0] // (ents // ent_dev)
    mine = lax.axis_index("z") * 2 + lax.axis_index("y")
    degrees = []
    for refs, count in (((own_first, other_first), 1), ((own_others, other_others), tiles - 1)):
        base = refs[0].shape[0] - 16
        parts = refs[0][base:, :].astype(F32) + refs[1][base:, :].astype(F32)
        degrees += [parts[2 * n : 2 * n + 1] + parts[2 * n + 1 : 2 * n + 2] for n in range(count)]
    for b in range(tiles):
        row = lax.rsqrt(1.0 + degrees[b])
        for h in range(TILE // 128):
            at = b * TILE + h * 128
            scale[at : at + 128, :] = row_to_column(row[:, h * 128 : (h + 1) * 128])
    square((own_first, other_first), (own_others, other_others), full)

    def es(at, rows):
        return jnp.concatenate([scale[at : at + rows, :]] * (width // 128), axis=1)

    def product(value, at, rows):
        return dot(full[at : at + rows, :], value[...])

    for at in range(0, ents, TILE):
        span = slice(at, at + TILE)
        values[span, :] = (es(at, TILE) * projected[span, :]).astype(BF)
    for at in range(0, ents, TILE):
        span = slice(at, at + TILE)
        preact = es(at, TILE) * product(values, at, TILE)
        gate = jax.nn.sigmoid(preact)
        acts[span, :] = (preact * gate).astype(BF)
        cot = cots[at // ent_dev * per_group : (at + TILE) // ent_dev * per_group].reshape(TILE, width).astype(F32)
        grad = cot * gate * (1.0 + preact * (1.0 - gate))
        backs[span, :] = (es(at, TILE) * grad).astype(BF)
    own_rows = pl.ds(pl.multiple_of(mine * ent_dev, ent_dev), ent_dev)
    activated[...] = acts[own_rows, :]
    for at in range(0, ents, TILE):
        acts[at : at + TILE, :] = (es(at, TILE) * product(backs, at, TILE)).astype(BF)
    grad_theta[...] = dot(feats[...].reshape(ents, width), acts[...], TN)
    grad_features[...] = dot(acts[own_rows, :], theta[...], NT).astype(BF)
    sections = incidence.shape[0]
    for q in range(0, sections, TILE):
        piece = incidence[q : q + TILE, :]
        both = dot(piece, values[...]) * dot(piece, backs[...])
        total = jnp.sum(both, axis=1, keepdims=True)
        grad_weight[:, q : q + TILE] = column_to_row(total) * inverse[:, q : q + TILE]


def dense_body(features, theta, section_weight, pair_rows, pair_cols, pair_counts, cotangent):
    ent_dev, width = features.shape
    sec_dev = section_weight.shape[0]
    _, blocks, slots = pair_rows.shape
    ents = blocks * ent_dev
    tiles = ents // TILE
    group = lax.axis_size("y") * lax.axis_size("x")
    layers = lax.axis_size("z")
    share = ent_dev // (lax.axis_size("x") * CORES)
    height = CHUNKS * 16 + 8
    swap = [(0, 1), (1, 0)]
    payload, inverse = pl.pallas_call(
        prep_kernel,
        out_shape=(
            jax.ShapeDtypeStruct((height + 4 * share, 128), BF),
            jax.ShapeDtypeStruct((1, sec_dev), F32),
        ),
        in_specs=[hbm()] * 6,
        out_specs=(vmem(), vmem()),
        scratch_shapes=[
            pltpu.SMEM((1, blocks), jnp.int32),
            pltpu.VMEM((blocks, slots), jnp.int32),
            pltpu.VMEM((blocks, slots), jnp.int32),
            pltpu.VMEM((1, sec_dev), F32),
            pltpu.VMEM((2 * share, width), BF),
            pltpu.SemaphoreType.DMA((6,)),
        ],
        compiler_params=params(63),
        name="prep",
    )(pair_counts, pair_rows, pair_cols, section_weight.reshape(1, sec_dev), features, cotangent)
    def layer(d):
        return lax.ppermute(payload, "z", [(i, i ^ d) for i in range(layers)])

    by_layer = [layer(d) for d in range(1, layers)]
    held = pl.pallas_call(
        hold_kernel,
        out_shape=jax.ShapeDtypeStruct(payload.shape, BF),
        in_specs=[vmem()],
        out_specs=vmem(),
        compiler_params=params(),
        name="hold",
    )(payload)
    rows = column_rows(ents)[-1][1]
    def step(kernel, shards, name, inputs):
        wide = shards * sec_dev
        return pl.pallas_call(
            kernel,
            out_shape=jax.ShapeDtypeStruct((rows, TILE), F32),
            in_specs=jax.tree.map(lambda _: vmem(), list(inputs)),
            out_specs=vmem(),
            scratch_shapes=[pltpu.VMEM((ents, wide), BF), pltpu.VMEM((ents + 16, wide), BF)],
            compiler_params=params(),
            cost_estimate=pl.CostEstimate(flops=1000000000, bytes_accessed=1000, transcendentals=0),
            name=name,
        )(*inputs)

    sums = step(own_kernel, 1, "gram_own", [held])
    sums, by_layer = lax.optimization_barrier((sums, by_layer))
    near = pl.pallas_call(
        collect_kernel,
        out_shape=jax.ShapeDtypeStruct((group,) + payload.shape, BF),
        in_specs=[vmem()] * 4,
        out_specs=vmem(),
        compiler_params=params(),
        name="collect",
    )(held, *by_layer)

    by_x, by_y = lax.ppermute(near, "x", swap), lax.ppermute(near, "y", swap)
    sums = step(layers_kernel, layers - 1, "gram_layers", [by_layer, sums])
    later, sums = lax.optimization_barrier((near, sums))
    by_both = lax.ppermute(later, ("y", "x"), [(i, i ^ 3) for i in range(group)])
    far = [near, by_x, by_y, by_both]
    pair = step(second_kernel, group, "gram_second", [far[1], sums])
    third, pair = lax.optimization_barrier((far[2], pair))
    single = step(third_kernel, group, "gram_third", [third])
    fourth, single = lax.optimization_barrier((far[3], single))

    def plain(kernel, outs, name, inputs):
        return pl.pallas_call(
            kernel,
            out_shape=[jax.ShapeDtypeStruct(shape, kind) for shape, kind in outs],
            in_specs=jax.tree.map(lambda _: vmem(), list(inputs)),
            out_specs=[vmem()] * len(outs),
            compiler_params=params(),
            cost_estimate=pl.CostEstimate(flops=1000000000, bytes_accessed=1000, transcendentals=0),
            name=name,
        )(*inputs)

    own_first, table, scaled = plain(
        last_kernel,
        [
            ((ents + layers * group * 2 * share + 16, TILE), BF),
            ((ents, group * sec_dev), BF),
            ((ents + 16, group * sec_dev), BF),
        ],
        "gram_last",
        [fourth, pair, single, tuple(far[:2]), third],
    )
    other_first = lax.ppermute(own_first, "core", swap)
    (own_others,) = plain(
        others_kernel, [((rows - 16 * tiles - ents + 16, TILE), BF)], "gram_others", [table, scaled, pair, single]
    )
    other_others = lax.ppermute(own_others, "core", swap)
    stack = (layers * group, CORES, share, width)
    incidence, feats, cots, projected = plain(
        middle_kernel,
        [((sec_dev, ents), BF), (stack, BF), (stack, BF), ((ents, width), F32)],
        "middle",
        [payload, own_first, other_first, theta],
    )
    tail_in = (own_first, own_others, other_first, other_others, feats, cots, projected, theta, incidence, inverse)
    activated, grad_features, grad_theta, grad_weight = pl.pallas_call(
        tail_kernel,
        out_shape=(
            jax.ShapeDtypeStruct((ent_dev, width), BF),
            jax.ShapeDtypeStruct((ent_dev, width), BF),
            jax.ShapeDtypeStruct((width, width), F32),
            jax.ShapeDtypeStruct((1, sec_dev), F32),
        ),
        in_specs=[vmem()] * len(tail_in),
        out_specs=(vmem(),) * 4,
        scratch_shapes=[
            pltpu.VMEM((ents, ents), BF),
            pltpu.VMEM((ents, 128), F32),
            pltpu.VMEM((ents, width), BF),
            pltpu.VMEM((ents, width), BF),
            pltpu.VMEM((ents, width), BF),
        ],
        compiler_params=params(),
        name="tail",
    )(*tail_in)
    return activated, grad_features, grad_theta, grad_weight.reshape(sec_dev)


def solution(mesh):
    ent, sec = mesh.shape["ent"], mesh.shape["sec"]
    dense = ent == 8 and sec == 4
    if dense:
        grid = Mesh(mesh.devices.reshape(ent // 2, 2, sec // CORES, CORES), ("z", "y", "x", "core"))
        whole, split = ("z", "y"), ("z", "y", "x", "core")
    else:
        grid = mesh
        whole, split = "ent", ("ent", "sec")
    placed = (
        P(whole, None),
        P(),
        P(split),
        P(split, None, None),
        P(split, None, None),
        P(split, None),
        P(whole, None),
    )
    return jax.shard_map(
        dense_body if dense else body,
        mesh=grid,
        in_specs=placed,
        out_specs=(P(whole, None), P(whole, None), P(), P(split)),
        check_vma=False,
    )
```

```python
import jax
import jax.numpy as jnp
from jax import lax
from jax.experimental import pallas as pl
from jax.experimental.pallas import tpu as pltpu
from jax.sharding import Mesh, PartitionSpec as P


def hot_table(indices, live_slots, offset, table_width):
    hits = (indices - offset)[:, None] == jnp.arange(table_width, dtype=jnp.int32)[None, :]
    return (hits & live_slots[:, None]).astype(jnp.bfloat16)


def body(features, theta, section_weight, pair_rows, pair_cols, pair_counts, cotangent):
    ent_dev = features.shape[0]
    feature_width = features.shape[1]
    sec_dev = section_weight.shape[0]
    blocks_count = pair_rows.shape[1]
    slot_count = pair_rows.shape[2]
    own_block = lax.axis_index("ent")
    row_lists = pair_rows[0]
    col_lists = pair_cols[0]
    usable = jnp.arange(slot_count, dtype=jnp.int32)[None, :] < pair_counts[0][:, None]
    usable_float = usable.astype(jnp.float32)
    entity_index = jnp.arange(blocks_count, dtype=jnp.int32)[:, None] * ent_dev + col_lists
    local_degree = jax.ops.segment_sum(
        usable_float.reshape(-1), entity_index.reshape(-1), num_segments=blocks_count * ent_dev
    )
    entity_degree = lax.psum(local_degree, ("ent", "sec"))
    own_degree = lax.dynamic_slice_in_dim(entity_degree, own_block * ent_dev, ent_dev)
    entity_scale = lax.rsqrt(1.0 + own_degree)[:, None]
    sec_count = jax.ops.segment_sum(
        usable_float.reshape(-1), row_lists.reshape(-1), num_segments=sec_dev
    )
    section_scale = (section_weight / (1.0 + sec_count))[:, None]

    def entity_fold(running, incoming, start_row):
        row_count = incoming.shape[0]
        span_width = min(row_count, ent_dev)
        block_span = max(row_count // ent_dev, 1)
        offset = start_row

        def add_block(turn_index, accum):
            row_slots = lax.dynamic_index_in_dim(row_lists, turn_index, 0, keepdims=False)
            col_slots = lax.dynamic_index_in_dim(col_lists, turn_index, 0, keepdims=False)
            live_slots = lax.dynamic_index_in_dim(usable, turn_index, 0, keepdims=False)
            values = lax.dynamic_slice_in_dim(incoming, turn_index * span_width, span_width, 0)
            col_hot = hot_table(col_slots, live_slots, offset, span_width)
            row_hot = hot_table(row_slots, live_slots, 0, sec_dev)
            picked = jnp.dot(col_hot, values, preferred_element_type=jnp.float32).astype(
                jnp.bfloat16
            )
            return accum + jnp.einsum(
                "ps,pf->sf", row_hot, picked, preferred_element_type=jnp.float32
            )

        return lax.fori_loop(0, block_span, add_block, running)

    def entity_terms(messages, start_row):
        span_width = min(lax.axis_size("ent") * ent_dev, ent_dev)
        block_span = max(lax.axis_size("ent") * ent_dev // ent_dev, 1)
        offset = start_row

        def block_term(turn_index):
            row_slots = lax.dynamic_index_in_dim(row_lists, turn_index, 0, keepdims=False)
            col_slots = lax.dynamic_index_in_dim(col_lists, turn_index, 0, keepdims=False)
            live_slots = lax.dynamic_index_in_dim(usable, turn_index, 0, keepdims=False)
            row_hot = hot_table(row_slots, live_slots, 0, sec_dev)
            col_hot = hot_table(col_slots, live_slots, offset, span_width)
            picked = jnp.dot(row_hot, messages, preferred_element_type=jnp.float32).astype(
                jnp.bfloat16
            )
            return jnp.einsum("pw,pf->wf", col_hot, picked, preferred_element_type=jnp.float32)

        pieces = lax.map(block_term, jnp.arange(block_span, dtype=jnp.int32))
        return pieces.reshape(block_span * span_width, feature_width)

    def collect(messages):
        partial_sum = lax.psum_scatter(
            entity_terms(messages, jnp.int32(0)), "ent", scatter_dimension=0, tiled=True
        )
        return lax.psum(partial_sum, "sec")

    zero_sections = jnp.zeros((sec_dev, feature_width), jnp.float32)
    projected = jnp.dot(features, theta, preferred_element_type=jnp.float32)
    scaled = (entity_scale * projected).astype(jnp.bfloat16)
    gathered = entity_fold(
        zero_sections, lax.all_gather(scaled, "ent", axis=0, tiled=True), jnp.int32(0)
    )
    messages = (section_scale * gathered).astype(jnp.bfloat16)
    collected = collect(messages)
    preact = entity_scale * collected
    activated = jax.nn.silu(preact).astype(jnp.bfloat16)
    sigmoid_pre = jax.nn.sigmoid(preact)
    grad_pre = cotangent.astype(jnp.float32) * sigmoid_pre * (1.0 + preact * (1.0 - sigmoid_pre))
    back_scaled = (entity_scale * grad_pre).astype(jnp.bfloat16)
    back_gathered = entity_fold(
        zero_sections, lax.all_gather(back_scaled, "ent", axis=0, tiled=True), jnp.int32(0)
    )
    grad_weight = jnp.sum(gathered * back_gathered, axis=1) / (1.0 + sec_count)
    back_messages = (section_scale * back_gathered).astype(jnp.bfloat16)
    back_collected = collect(back_messages)
    grad_proj = (entity_scale * back_collected).astype(jnp.bfloat16)
    grad_features = lax.dot_general(
        grad_proj, theta, (((1,), (1,)), ((), ())), preferred_element_type=jnp.float32
    ).astype(jnp.bfloat16)
    local_theta = lax.dot_general(
        features, grad_proj, (((0,), (0,)), ((), ())), preferred_element_type=jnp.float32
    )
    grad_theta = lax.psum(local_theta, "ent")
    return (activated, grad_features, grad_theta, grad_weight)


BF = jnp.bfloat16
F32 = jnp.float32
BIT = jnp.float8_e4m3fn
TILE = 256
SHIFT = TILE.bit_length() - 1
NT = (((1,), (1,)), ((), ()))
TN = (((0,), (0,)), ((), ()))
CORES = 2
CHUNKS = 4


def params(mebibytes=32):
    return pltpu.CompilerParams(vmem_limit_bytes=mebibytes * 2**20)


def vmem():
    return pl.BlockSpec(memory_space=pltpu.VMEM)


def hbm():
    return pl.BlockSpec(memory_space=pltpu.HBM)


def dot(a, b, dims=(((1,), (0,)), ((), ()))):
    return lax.dot_general(a, b, dims, preferred_element_type=F32)


def one_hot(index_row, count=TILE):
    ids = lax.broadcasted_iota(jnp.int32, (count, index_row.shape[1]), 0).astype(BF)
    return jnp.where(ids == index_row, jnp.ones((), BIT), jnp.zeros((), BIT))


def index_hot(lists, j, chunks):
    parts = [one_hot(lists[16 * c + j : 16 * c + j + 1, :]) for c in range(chunks)]
    return jnp.concatenate(parts, axis=1)


def column_to_row(column):
    wide = jnp.broadcast_to(column, (column.shape[0], 128))
    return wide.T[0:1, :]


def row_to_column(row):
    return jnp.broadcast_to(row, (128, 128)).T


def prep_kernel(
    counts, rows, cols, weight, features, cotangent, payload, inverse,
    counts_here, rows_here, cols_here, weight_here, share_here, sems,
):
    _, blocks, slots = rows.shape
    chunks = slots // 128
    ent_dev = features.shape[0]
    share = share_here.shape[0] // 2
    quarter = lax.axis_index("x") * CORES + lax.axis_index("core")
    here = pl.ds(pl.multiple_of(quarter * share, share), share)
    reads = [
        pltpu.make_async_copy(source, target, sems.at[n])
        for n, (source, target) in enumerate(
            (
                (counts, counts_here),
                (rows.at[0], rows_here),
                (cols.at[0], cols_here),
                (weight, weight_here),
                (features.at[here, :], share_here.at[0:share, :]),
                (cotangent.at[here, :], share_here.at[share : 2 * share, :]),
            )
        )
    ]
    for read in reads:
        read.start()
    for read in reads:
        read.wait()
    row_ids = rows_here[...]
    sub = lax.broadcasted_iota(jnp.int32, (blocks, slots), 0)
    lane = lax.broadcasted_iota(jnp.int32, (blocks, slots), 1)
    limit = jnp.zeros((blocks, slots), jnp.int32)
    for j in range(blocks):
        limit = jnp.where(sub == j, counts_here[0, j], limit)
    live = lane < limit
    part = lax.shift_right_logical(row_ids, SHIFT)
    high = jnp.where(live, part * ent_dev + cols_here[...], -1).astype(F32)
    low = jnp.where(live, row_ids & (TILE - 1), -1).astype(F32)
    chunk = lax.shift_right_logical(row_ids, 7).astype(F32)
    place = jnp.where(live, row_ids & 127, -1).astype(F32)
    degree = jnp.zeros((16, 128), F32)
    for j in range(blocks):
        degree = degree + dot(
            one_hot(chunk[j : j + 1].astype(BF), 16), one_hot(place[j : j + 1].astype(BF), 128), NT
        )
    degree = jnp.concatenate([degree[c : c + 1] for c in range(weight.shape[1] // 128)], axis=1)
    inverse[...] = 1.0 / (1.0 + degree)
    scale = weight_here[...] / (1.0 + degree)
    indices = jnp.concatenate([high, low], axis=0).astype(BF)
    for c in range(chunks):
        payload[16 * c : 16 * (c + 1), :] = indices[:, 128 * c : 128 * (c + 1)]
    ends = [scale[:, 128 * c : 128 * (c + 1)] for c in range(chunks)]
    ends.append(jnp.zeros((8 - chunks, 128), F32))
    at = 16 * chunks
    payload[at : at + 8, :] = jnp.concatenate(ends, axis=0).astype(BF)
    at += 8
    for n in range(2):
        for half in range(2):
            payload[at : at + share, :] = share_here[n * share : (n + 1) * share, half * 128 : (half + 1) * 128]
            at += share


def hold_kernel(source, target):
    target[...] = source[...]


def square(firsts, others, full):
    ents = full.shape[0]
    start = 0
    for b in range(0, ents, TILE):
        for a in range(b, ents, TILE):
            refs, at = (firsts, a) if b == 0 else (others, start)
            parts = [ref[at : at + TILE, :].astype(F32) for ref in refs]
            piece = (parts[0] + parts[1]).astype(BF)
            full[a : a + TILE, b : b + TILE] = piece
            if a != b:
                full[b : b + TILE, a : a + TILE] = piece.T
            start += TILE if b else 0


def middle_kernel(payload, own_first, other_first, theta, incidence, feats, cots, projected):
    ents = incidence.shape[1]
    ent_dev = TILE // (incidence.shape[0] // TILE)
    chunks = CHUNKS
    share = feats.shape[2]
    core = lax.axis_index("core")
    columns = lax.axis_size("y") * lax.axis_size("x")
    column_here = lax.axis_index("y") * 2 + lax.axis_index("x")
    for n, source in enumerate((own_first, other_first)):
        which = core if n == 0 else 1 - core
        at = ents
        for d in range(columns):
            there = jnp.bitwise_xor(column_here, d)
            for q in range(feats.shape[0] // columns):
                feats[q * columns + there, which] = source[at : at + share, :]
                cots[q * columns + there, which] = source[at + share : at + 2 * share, :]
                at += 2 * share
    for j in range(ents // ent_dev):
        block = dot(index_hot(payload, 8 + j, chunks), index_hot(payload, j, chunks), NT).astype(BF)
        for half in range(2):
            incidence[half * TILE : (half + 1) * TILE, j * ent_dev : (j + 1) * ent_dev] = block[
                :, half * ent_dev : (half + 1) * ent_dev
            ]
    every = feats[...].reshape(ents, theta.shape[0])
    projected[...] = dot(every, theta[...])


def collect_kernel(own, first, second, third, group):
    mine = lax.axis_index("z")
    for d, source in enumerate((own, first, second, third)):
        group[jnp.bitwise_xor(mine, d)] = source[...]


def column_rows(ents):
    spans, start = [], 0
    for b in range(ents // TILE):
        end = start + ents - b * TILE + 16
        spans.append((start, end))
        start = end
    return spans


def members(group):
    return [group.at[q] for q in range(group.shape[0])]


def fill(shards, table, scaled):
    chunks = CHUNKS
    ents = table.shape[0]
    sections = table.shape[1] // len(shards)
    ent_dev = TILE // (sections // TILE)
    scaled[ents:, :] = jnp.ones((scaled.shape[0] - ents, scaled.shape[1]), BF)
    for q, indices in enumerate(shards):
        scale = jnp.concatenate(
            [indices[16 * chunks + c : 16 * chunks + c + 1, :] for c in range(chunks)], axis=1
        )
        for j in range(ents // ent_dev):
            block = dot(index_hot(indices, j, chunks), index_hot(indices, 8 + j, chunks), NT).astype(BF)
            rows = slice(j * ent_dev, (j + 1) * ent_dev)
            for half in range(2):
                at = q * sections + half * TILE
                part = block[half * ent_dev : (half + 1) * ent_dev, :]
                table[rows, at : at + TILE] = part
                scaled[rows, at : at + TILE] = part * scale[:, half * TILE : (half + 1) * TILE]


def column(b, table, scaled):
    return dot(scaled[b * TILE :, :], table[b * TILE : (b + 1) * TILE, :], NT)


def shards_kernel(shards, sums, table, scaled):
    fill(shards, table, scaled)
    for b, (start, end) in enumerate(column_rows(table.shape[0])):
        sums[start:end, :] = column(b, table, scaled)


def own_kernel(payload, sums, table, scaled):
    shards_kernel([payload], sums, table, scaled)


def third_kernel(group, sums, table, scaled):
    shards_kernel(members(group), sums, table, scaled)


def layers_kernel(arrived, before, sums, table, scaled):
    fill(arrived, table, scaled)
    for b, (start, end) in enumerate(column_rows(table.shape[0])):
        sums[start:end, :] = before[start:end, :] + column(b, table, scaled)


def second_kernel(group, before, sums, table, scaled):
    layers_kernel(members(group), before, sums, table, scaled)


def degree_rows(*rows):
    out = []
    for row in rows:
        top = row.astype(BF).astype(F32)
        out += [top, row - top]
    out.append(jnp.zeros((16 - len(out), TILE), F32))
    return jnp.concatenate(out, axis=0).astype(BF)


def last_kernel(lists, pair, single, near, third, first, table, scaled):
    ents = table.shape[0]
    fill(members(lists), table, scaled)
    start, end = column_rows(ents)[0]
    total = pair[start:end, :] + (single[start:end, :] + column(0, table, scaled))
    first[0:ents, :] = total[0:ents].astype(BF)
    first[first.shape[0] - 16 :, :] = degree_rows(total[ents : ents + 1])
    at = ents
    for source in near + (third, lists):
        shards, height, _ = source.shape
        top = 16 * CHUNKS + 8
        share = (height - top) // 4
        for q in range(shards):
            for k in range(4):
                rows = slice(at + k // 2 * share, at + (k // 2 + 1) * share)
                first[rows, k % 2 * 128 : k % 2 * 128 + 128] = source[q, top + k * share : top + (k + 1) * share, :]
            at += 2 * share


def others_kernel(table, scaled, pair, single, others):
    ents = table.shape[0]
    at = 0
    degrees = []
    for b, (start, end) in enumerate(column_rows(ents)):
        if b:
            size = end - start - 16
            total = pair[start:end, :] + (single[start:end, :] + column(b, table, scaled))
            others[at : at + size, :] = total[0:size].astype(BF)
            at += size
            degrees.append(total[size : size + 1])
    others[at : at + 16, :] = degree_rows(*degrees)


def tail_kernel(
    own_first, own_others, other_first, other_others, feats, cots, projected, theta, incidence, inverse,
    activated, grad_features, grad_theta, grad_weight,
    full, scale, values, backs, acts,
):
    ents = full.shape[0]
    tiles = ents // TILE
    ent_dev = activated.shape[0]
    width = theta.shape[0]
    per_group = feats.shape[0] // (ents // ent_dev)
    mine = lax.axis_index("z") * 2 + lax.axis_index("y")
    degrees = []
    for refs, count in (((own_first, other_first), 1), ((own_others, other_others), tiles - 1)):
        base = refs[0].shape[0] - 16
        parts = refs[0][base:, :].astype(F32) + refs[1][base:, :].astype(F32)
        degrees += [parts[2 * n : 2 * n + 1] + parts[2 * n + 1 : 2 * n + 2] for n in range(count)]
    for b in range(tiles):
        row = lax.rsqrt(1.0 + degrees[b])
        for h in range(TILE // 128):
            at = b * TILE + h * 128
            scale[at : at + 128, :] = row_to_column(row[:, h * 128 : (h + 1) * 128])
    square((own_first, other_first), (own_others, other_others), full)

    def es(at, rows):
        return jnp.concatenate([scale[at : at + rows, :]] * (width // 128), axis=1)

    def product(value, at, rows):
        return dot(full[at : at + rows, :], value[...])

    for at in range(0, ents, TILE):
        span = slice(at, at + TILE)
        values[span, :] = (es(at, TILE) * projected[span, :]).astype(BF)
    for at in range(0, ents, TILE):
        span = slice(at, at + TILE)
        preact = es(at, TILE) * product(values, at, TILE)
        gate = jax.nn.sigmoid(preact)
        acts[span, :] = (preact * gate).astype(BF)
        cot = cots[at // ent_dev * per_group : (at + TILE) // ent_dev * per_group].reshape(TILE, width).astype(F32)
        grad = cot * gate * (1.0 + preact * (1.0 - gate))
        backs[span, :] = (es(at, TILE) * grad).astype(BF)
    own_rows = pl.ds(pl.multiple_of(mine * ent_dev, ent_dev), ent_dev)
    activated[...] = acts[own_rows, :]
    for at in range(0, ents, TILE):
        acts[at : at + TILE, :] = (es(at, TILE) * product(backs, at, TILE)).astype(BF)
    grad_theta[...] = dot(feats[...].reshape(ents, width), acts[...], TN)
    grad_features[...] = dot(acts[own_rows, :], theta[...], NT).astype(BF)
    sections = incidence.shape[0]
    for q in range(0, sections, TILE):
        piece = incidence[q : q + TILE, :]
        both = dot(piece, values[...]) * dot(piece, backs[...])
        total = jnp.sum(both, axis=1, keepdims=True)
        grad_weight[:, q : q + TILE] = column_to_row(total) * inverse[:, q : q + TILE]


def dense_body(features, theta, section_weight, pair_rows, pair_cols, pair_counts, cotangent):
    ent_dev, width = features.shape
    sec_dev = section_weight.shape[0]
    _, blocks, slots = pair_rows.shape
    ents = blocks * ent_dev
    tiles = ents // TILE
    group = lax.axis_size("y") * lax.axis_size("x")
    layers = lax.axis_size("z")
    share = ent_dev // (lax.axis_size("x") * CORES)
    height = CHUNKS * 16 + 8
    swap = [(0, 1), (1, 0)]
    payload, inverse = pl.pallas_call(
        prep_kernel,
        out_shape=(
            jax.ShapeDtypeStruct((height + 4 * share, 128), BF),
            jax.ShapeDtypeStruct((1, sec_dev), F32),
        ),
        in_specs=[hbm()] * 6,
        out_specs=(vmem(), vmem()),
        scratch_shapes=[
            pltpu.SMEM((1, blocks), jnp.int32),
            pltpu.VMEM((blocks, slots), jnp.int32),
            pltpu.VMEM((blocks, slots), jnp.int32),
            pltpu.VMEM((1, sec_dev), F32),
            pltpu.VMEM((2 * share, width), BF),
            pltpu.SemaphoreType.DMA((6,)),
        ],
        compiler_params=params(63),
        name="prep",
    )(pair_counts, pair_rows, pair_cols, section_weight.reshape(1, sec_dev), features, cotangent)
    def layer(d):
        return lax.ppermute(payload, "z", [(i, i ^ d) for i in range(layers)])

    by_layer = [layer(d) for d in range(1, layers)]
    held = pl.pallas_call(
        hold_kernel,
        out_shape=jax.ShapeDtypeStruct(payload.shape, BF),
        in_specs=[vmem()],
        out_specs=vmem(),
        compiler_params=params(),
        name="hold",
    )(payload)
    rows = column_rows(ents)[-1][1]
    def step(kernel, shards, name, inputs):
        wide = shards * sec_dev
        return pl.pallas_call(
            kernel,
            out_shape=jax.ShapeDtypeStruct((rows, TILE), F32),
            in_specs=jax.tree.map(lambda _: vmem(), list(inputs)),
            out_specs=vmem(),
            scratch_shapes=[pltpu.VMEM((ents, wide), BF), pltpu.VMEM((ents + 16, wide), BF)],
            compiler_params=params(),
            cost_estimate=pl.CostEstimate(flops=1000000000, bytes_accessed=1000, transcendentals=0),
            name=name,
        )(*inputs)

    sums = step(own_kernel, 1, "gram_own", [held])
    sums, by_layer = lax.optimization_barrier((sums, by_layer))
    near = pl.pallas_call(
        collect_kernel,
        out_shape=jax.ShapeDtypeStruct((group,) + payload.shape, BF),
        in_specs=[vmem()] * 4,
        out_specs=vmem(),
        compiler_params=params(),
        name="collect",
    )(held, *by_layer)

    by_x, by_y = lax.ppermute(near, "x", swap), lax.ppermute(near, "y", swap)
    sums = step(layers_kernel, layers - 1, "gram_layers", [by_layer, sums])
    later, sums = lax.optimization_barrier((near, sums))
    by_both = lax.ppermute(later, ("y", "x"), [(i, i ^ 3) for i in range(group)])
    far = [near, by_x, by_y, by_both]
    pair = step(second_kernel, group, "gram_second", [far[1], sums])
    third, pair = lax.optimization_barrier((far[2], pair))
    single = step(third_kernel, group, "gram_third", [third])
    fourth, single = lax.optimization_barrier((far[3], single))

    def plain(kernel, outs, name, inputs):
        return pl.pallas_call(
            kernel,
            out_shape=[jax.ShapeDtypeStruct(shape, kind) for shape, kind in outs],
            in_specs=jax.tree.map(lambda _: vmem(), list(inputs)),
            out_specs=[vmem()] * len(outs),
            compiler_params=params(),
            cost_estimate=pl.CostEstimate(flops=1000000000, bytes_accessed=1000, transcendentals=0),
            name=name,
        )(*inputs)

    own_first, table, scaled = plain(
        last_kernel,
        [
            ((ents + layers * group * 2 * share + 16, TILE), BF),
            ((ents, group * sec_dev), BF),
            ((ents + 16, group * sec_dev), BF),
        ],
        "gram_last",
        [fourth, pair, single, tuple(far[:2]), third],
    )
    other_first = lax.ppermute(own_first, "core", swap)
    (own_others,) = plain(
        others_kernel, [((rows - 16 * tiles - ents + 16, TILE), BF)], "gram_others", [table, scaled, pair, single]
    )
    other_others = lax.ppermute(own_others, "core", swap)
    stack = (layers * group, CORES, share, width)
    incidence, feats, cots, projected = plain(
        middle_kernel,
        [((sec_dev, ents), BF), (stack, BF), (stack, BF), ((ents, width), F32)],
        "middle",
        [payload, own_first, other_first, theta],
    )
    tail_in = (own_first, own_others, other_first, other_others, feats, cots, projected, theta, incidence, inverse)
    activated, grad_features, grad_theta, grad_weight = pl.pallas_call(
        tail_kernel,
        out_shape=(
            jax.ShapeDtypeStruct((ent_dev, width), BF),
            jax.ShapeDtypeStruct((ent_dev, width), BF),
            jax.ShapeDtypeStruct((width, width), F32),
            jax.ShapeDtypeStruct((1, sec_dev), F32),
        ),
        in_specs=[vmem()] * len(tail_in),
        out_specs=(vmem(),) * 4,
        scratch_shapes=[
            pltpu.VMEM((ents, ents), BF),
            pltpu.VMEM((ents, 128), F32),
            pltpu.VMEM((ents, width), BF),
            pltpu.VMEM((ents, width), BF),
            pltpu.VMEM((ents, width), BF),
        ],
        compiler_params=params(),
        name="tail",
    )(*tail_in)
    return activated, grad_features, grad_theta, grad_weight.reshape(sec_dev)


def solution(mesh):
    ent, sec = mesh.shape["ent"], mesh.shape["sec"]
    dense = ent == 8 and sec == 4
    if dense:
        grid = Mesh(mesh.devices.reshape(ent // 2, 2, sec // CORES, CORES), ("z", "y", "x", "core"))
        whole, split = ("z", "y"), ("z", "y", "x", "core")
    else:
        grid = mesh
        whole, split = "ent", ("ent", "sec")
    placed = (
        P(whole, None),
        P(),
        P(split),
        P(split, None, None),
        P(split, None, None),
        P(split, None),
        P(whole, None),
    )
    return jax.shard_map(
        dense_body if dense else body,
        mesh=grid,
        in_specs=placed,
        out_specs=(P(whole, None), P(whole, None), P(), P(split)),
        check_vma=False,
    )
```
